256 devices in a mesh: tok: 32 (over x, z), head: 8 (over y, core).
Axes of the slice: x: 4, y: 4, z: 8, core: 2. Of those that a mesh axis runs over, the one named last changes fastest.
Arguments:
- queries: bfloat16 [32768, 4096], P(('tok', 'head')), may hold values from -32 to 32
- key_states: bfloat16 [32768, 512], P(('tok', 'head')), may hold values from -10 to 10
- value_states: bfloat16 [32768, 512], P(('tok', 'head')), may hold values from -6 to 6
- out_grad: bfloat16 [32768, 4096], P(('tok', 'head')), may hold values from -15 to 15
- sink_logits: float32 [64], P('head'), may hold values from 0 to 5
- branch_start: int32 [64], replicated, may hold values from 0 to 32640, as said below
- branch_len: int32 [64], replicated, may hold values from 128 to 384, as said below
- parent_list: int32 [64, 2], replicated, may hold values from -1 to 256, as said below
Outputs:
- attn_out: bfloat16 [32768, 4096], P(('tok', 'head'))
- query_grad: bfloat16 [32768, 4096], P(('tok', 'head'))
- key_grad: bfloat16 [32768, 512], P(('tok', 'head'))
- value_grad: bfloat16 [32768, 512], P(('tok', 'head'))
- sink_grad: float32 [64], P('head')
The draws below stay inside these ranges and needn't reach their ends.
Inputs may be any that keep to these rules, and one draw needn't show every extreme that they name: `branch_start`: branch b lies within the tokens of index b // 2 of tok. The branches of one index follow one another in order, begin at multiples of 128 and do not intersect; tokens between them belong to no branch. `branch_len`: A multiple of 128. `parent_list`: row b is (parent branch, tail offset). The branches of index 0 of tok have parent -1 and offset 0; the parent of a branch on index d lies on index d - s for some s from 1 to min(3, d), and each s from 1 to 3 occurs. Branches 2m and 2m + 1 are siblings with equal rows. The offset is a multiple of 128 and the 128 tokens of the parent that begin there lie inside the parent.
All inputs are finite; a program needn't handle non-finite values.
Results may differ from the reference program's by a relative error of at most 0.02.
Values may be sent and summed in bfloat16 or wider, within the bound.
A program may use at most 64 MiB of HBM per device.

```python
import math
import jax
import jax.numpy as jnp
from jax import lax

HEAD_DIM = 64
Q_HEADS = 64
KV_HEADS = 8
WINDOW = 128
LAG = 3
BLK_DEV = 8
BR_DEV = 2
PAIRS = 1
BRANCHES = 64
TOKENS = 32768
N_TOK = 32


def tree_layout(key):
    length_key, gap_key = jax.random.split(key, 2)
    spans = jax.random.randint(length_key, (N_TOK, BR_DEV), 1, 4)
    last_col = jnp.arange(BR_DEV)[None, :] == BR_DEV - 1
    spans = jnp.where(last_col, 3, spans)
    gaps = jax.random.randint(gap_key, (N_TOK, BR_DEV), 0, 2)
    ends = jnp.cumsum(spans + gaps, axis=1)
    offsets = ends - spans + jnp.arange(N_TOK)[:, None] * BLK_DEV
    return ((offsets * WINDOW).reshape(-1).astype(jnp.int32), (spans * WINDOW).reshape(-1).astype(jnp.int32), spans.reshape(-1))


def scaled_rows(value_key, scale_key, heads, low, high):
    scales = jnp.exp(jax.random.uniform(scale_key, (TOKENS, heads, 1), minval=math.log(low), maxval=math.log(high)))
    values = jnp.clip(jax.random.normal(value_key, (TOKENS, heads, HEAD_DIM)), -4.0, 4.0)
    return (values * scales).reshape(TOKENS, heads * HEAD_DIM)


def draw_branch_start(key, part):
    starts, lengths, spans = tree_layout(key)
    return starts


def draw_branch_len(key, part):
    starts, lengths, spans = tree_layout(key)
    return lengths


def draw_parent_list(key, part):
    starts, lengths, spans = tree_layout(key)
    key = jax.random.fold_in(key, 3)
    lag_key, pick_key, offset_key = jax.random.split(key, 3)
    count = N_TOK * BR_DEV
    device_ids = jnp.arange(N_TOK, dtype=jnp.int32)[:, None]
    pair_ids = jnp.arange(PAIRS, dtype=jnp.int32)[None, :]
    pinned = (device_ids == N_TOK - 1) & (pair_ids == 0)
    reach = jnp.maximum(jnp.minimum(device_ids, LAG), 1)
    rolls = jax.random.randint(lag_key, (N_TOK, PAIRS), 0, 36)
    distance = jnp.where(pair_ids == 0, 1 + device_ids % reach, 1 + rolls % reach)
    distance = jnp.where(pinned, 1, distance)
    owner = device_ids - distance
    picks_branch = jax.random.randint(pick_key, (N_TOK, PAIRS), 0, BR_DEV)
    picks_branch = jnp.where(pinned, BR_DEV - 1, picks_branch)
    parents = owner * BR_DEV + picks_branch
    rooted = device_ids == 0
    parents = jnp.where(rooted, -1, parents)
    parent_spans = spans[jnp.maximum(parents, 0)]
    picks = jax.random.randint(offset_key, (N_TOK, PAIRS), 0, 168)
    offsets = jnp.where(rooted, 0, picks % parent_spans * WINDOW)
    offsets = jnp.where(pinned, 2 * WINDOW, offsets)
    both = jnp.stack([parents, offsets], axis=-1)
    return jnp.repeat(both, 2, axis=1).reshape(count, 2).astype(jnp.int32)


def draw_key_states(key, part):
    key = jax.random.fold_in(key, 11)
    value_key, scale_key = jax.random.split(key)
    return scaled_rows(value_key, scale_key, KV_HEADS, 0.4, 2.5).astype(jnp.bfloat16)


def draw_queries(key, part):
    key = jax.random.fold_in(key, 13)
    value_key, scale_key = jax.random.split(key)
    return scaled_rows(value_key, scale_key, Q_HEADS, 0.4, 2.5).astype(jnp.bfloat16)


def draw_out_grad(key, part):
    key = jax.random.fold_in(key, 5)
    ramp = jnp.arange(TOKENS, dtype=jnp.float32)[:, None] / TOKENS
    values = jnp.clip(jax.random.normal(key, (TOKENS, Q_HEADS * HEAD_DIM)), -5.0, 5.0)
    return (values * (1.0 + 2.0 * ramp)).astype(jnp.bfloat16)


def level_of(own_key, extent, cuts, smallest, high):
    def one(position, shards_of):
        steps = jax.random.uniform(jax.random.fold_in(jax.random.fold_in(own_key, 6), position), (shards_of,), jnp.float32, smallest / len(cuts), high / len(cuts))
        return jnp.repeat(jnp.exp(steps), extent[position] // shards_of).reshape((-1,) + (1,) * (len(extent) - position - 1))

    loudness = one(*cuts[0])
    for cut in cuts[1:]:
        loudness = loudness * one(*cut)
    return loudness


def normal_values(stream_key, dims, deviation, most, cuts=(), kind=jnp.bfloat16):
    values = deviation * jax.random.normal(stream_key, dims, jnp.float32)
    if cuts:
        values = values * level_of(stream_key, dims, cuts, -0.22, 0.18)
    return jnp.clip(values, -most, most).astype(kind)


def setup_inputs(seed: int = 0) -> dict:
    key_list = jax.random.split(jax.random.key(seed), 9)
    queries = draw_queries(jax.random.fold_in(key_list[8], 71), 0)
    key_states = draw_key_states(jax.random.fold_in(key_list[8], 71), 0)
    value_states = normal_values(key_list[2], (TOKENS, KV_HEADS * HEAD_DIM), 1.0, 6.0, ((0, 256),))
    out_grad = draw_out_grad(jax.random.fold_in(key_list[8], 71), 0)
    sink_logits = jnp.clip(5.0 * jax.random.uniform(key_list[4], (Q_HEADS,), jnp.float32) ** level_of(key_list[4], (Q_HEADS,), ((0, 8),), -0.2, 0.2), 0.0, 5.0)
    branch_start = draw_branch_start(jax.random.fold_in(key_list[8], 71), 0)
    branch_len = draw_branch_len(jax.random.fold_in(key_list[8], 71), 0)
    parent_list = draw_parent_list(jax.random.fold_in(key_list[8], 71), 0)
    return dict(queries=queries, key_states=key_states, value_states=value_states, out_grad=out_grad, sink_logits=sink_logits, branch_start=branch_start, branch_len=branch_len, parent_list=parent_list)


def product(spec, left, right):
    return jnp.einsum(spec, left.astype(jnp.float32), right.astype(jnp.float32))

def attend(query_rows, key_own, value_own, key_prev, value_prev, grad_rows, prev_ok, alive, sink_table):
    window_len = query_rows.shape[1]
    factor = 1.0 / math.sqrt(query_rows.shape[-1])
    offsets = jnp.arange(window_len)
    causal = offsets[None, :] <= offsets[:, None]
    behind = (offsets[None, :] > offsets[:, None])[None, None, None] & prev_ok[:, None, None, None, None]
    own_scores = jnp.where(causal, product('bqkgd,bjkd->bkgqj', query_rows, key_own) * factor, -jnp.inf)
    prev_scores = jnp.where(behind, product('bqkgd,bjkd->bkgqj', query_rows, key_prev) * factor, -jnp.inf)
    sink_col = sink_table[None, :, :, None]
    peak = jnp.maximum(jnp.maximum(lax.optimization_barrier(jnp.max(own_scores, axis=-1)), lax.optimization_barrier(jnp.max(prev_scores, axis=-1))), sink_col)
    own_exp = jnp.exp(own_scores - peak[..., None])
    prev_exp = jnp.exp(prev_scores - peak[..., None])
    sink_exp = jnp.exp(sink_col - peak)
    summed = lax.optimization_barrier(jnp.sum(own_exp, axis=-1)) + lax.optimization_barrier(jnp.sum(prev_exp, axis=-1)) + sink_exp
    own_prob = own_exp / summed[..., None]
    prev_prob = prev_exp / summed[..., None]
    own_half = own_prob.astype(jnp.bfloat16)
    prev_half = prev_prob.astype(jnp.bfloat16)
    blended = product('bkgqj,bjkd->bqkgd', own_half, value_own) + product('bkgqj,bjkd->bqkgd', prev_half, value_prev)
    alive_rows = alive[:, None, None, None, None]
    attended = jnp.where(alive_rows, blended, 0.0).astype(jnp.bfloat16)
    grad_rows = jnp.where(alive_rows, grad_rows, jnp.zeros_like(grad_rows))
    row_delta = jnp.moveaxis(lax.optimization_barrier(jnp.sum(grad_rows.astype(jnp.float32) * attended.astype(jnp.float32), axis=-1)), 1, -1)
    own_slope = (own_prob * (product('bqkgd,bjkd->bkgqj', grad_rows, value_own) - row_delta[..., None])).astype(jnp.bfloat16)
    prev_slope = (prev_prob * (product('bqkgd,bjkd->bkgqj', grad_rows, value_prev) - row_delta[..., None])).astype(jnp.bfloat16)
    query_grad = ((product('bkgqj,bjkd->bqkgd', own_slope, key_own) + product('bkgqj,bjkd->bqkgd', prev_slope, key_prev)) * factor).astype(jnp.bfloat16)
    key_own_grad = product('bkgqj,bqkgd->bjkd', own_slope, query_rows) * factor
    key_prev_grad = product('bkgqj,bqkgd->bjkd', prev_slope, query_rows) * factor
    value_own_grad = product('bkgqj,bqkgd->bjkd', own_half, grad_rows)
    value_prev_grad = product('bkgqj,bqkgd->bjkd', prev_half, grad_rows)
    sink_grad = -lax.optimization_barrier(jnp.sum(sink_exp / summed * row_delta, axis=(0, 3)))
    return (attended, query_grad, key_own_grad, value_own_grad, key_prev_grad, value_prev_grad, sink_grad)

def reference(queries, key_states, value_states, out_grad, sink_logits, branch_start, branch_len, parent_list):
    blocks = TOKENS // WINDOW
    branch_ids = jnp.arange(BRANCHES, dtype=jnp.int32)
    block_pos = jnp.arange(blocks, dtype=jnp.int32) * WINDOW
    branch_end = branch_start + branch_len
    covers = (branch_start[None, :] <= block_pos[:, None]) & (block_pos[:, None] < branch_end[None, :])
    alive = jnp.any(covers, axis=1)
    opening = jnp.any(covers & (branch_start[None, :] == block_pos[:, None]), axis=1)
    holder = lax.optimization_barrier(jnp.sum(jnp.where(covers, branch_ids[None, :], 0), axis=1)).astype(jnp.int32)
    parent = parent_list[:, 0]
    parent_start = lax.optimization_barrier(jnp.sum(jnp.where(branch_ids[None, :] == parent[:, None], branch_start[None, :], 0), axis=1))
    tail_block = ((parent_start + parent_list[:, 1]) // WINDOW).astype(jnp.int32)
    has_tail = parent >= 0
    prev_block = jnp.where(opening, tail_block[holder], jnp.arange(blocks, dtype=jnp.int32) - 1)
    prev_ok = alive & (jnp.logical_not(opening) | has_tail[holder])
    prev_block = jnp.where(prev_ok, prev_block, 0).astype(jnp.int32)
    group_size = Q_HEADS // KV_HEADS
    query_blocks = queries.reshape(blocks, WINDOW, KV_HEADS, group_size, HEAD_DIM)
    grad_blocks = out_grad.reshape(blocks, WINDOW, KV_HEADS, group_size, HEAD_DIM)
    key_blocks = key_states.reshape(blocks, WINDOW, KV_HEADS, HEAD_DIM)
    value_blocks = value_states.reshape(blocks, WINDOW, KV_HEADS, HEAD_DIM)
    key_before = key_blocks[prev_block]
    value_before = value_blocks[prev_block]
    sink_table = sink_logits.reshape(KV_HEADS, group_size).astype(jnp.float32)
    per_stretch = blocks // N_TOK

    def split_stretches(array):
        return array.reshape((N_TOK, per_stretch) + array.shape[1:])

    def attend_stretch(pieces):
        return attend(*pieces, sink_table)
    results = lax.map(attend_stretch, (split_stretches(query_blocks), split_stretches(key_blocks), split_stretches(value_blocks), split_stretches(key_before), split_stretches(value_before), split_stretches(grad_blocks), split_stretches(prev_ok), split_stretches(alive)))
    attended, query_grad, key_own, value_own, key_prev, value_prev, sink_parts = results

    def merge_stretches(array):
        return array.reshape((blocks,) + array.shape[2:])
    keep = prev_ok[:, None, None, None]
    key_total = merge_stretches(key_own).at[prev_block].add(jnp.where(keep, merge_stretches(key_prev), 0.0))
    value_total = merge_stretches(value_own).at[prev_block].add(jnp.where(keep, merge_stretches(value_prev), 0.0))
    return (merge_stretches(attended).reshape(TOKENS, Q_HEADS * HEAD_DIM), merge_stretches(query_grad).reshape(TOKENS, Q_HEADS * HEAD_DIM), key_total.astype(jnp.bfloat16).reshape(TOKENS, KV_HEADS * HEAD_DIM), value_total.astype(jnp.bfloat16).reshape(TOKENS, KV_HEADS * HEAD_DIM), lax.optimization_barrier(jnp.sum(sink_parts, axis=0)).reshape(Q_HEADS))
```

```python
import functools

import jax
import jax.numpy as jnp
from jax import lax
from jax.experimental import pallas as pl
from jax.experimental.pallas import tpu as pltpu
from jax.sharding import PartitionSpec as P

HEAD_DIM = 64
WINDOW = 128
LAG = 3
BR_DEV = 2
GROUP = 8
RING = 32
ROWS = WINDOW // GROUP
KV = 512
Z = 8
X = 4
F32 = jnp.float32
BF16 = jnp.bfloat16
MESH = pl.DeviceIdType.MESH


def place():
    return lax.axis_index("tok"), lax.axis_index("head")


def block_state(tok, head, start, length, parent):
    pos = (tok * GROUP + head) * WINDOW
    alive, opening = False, False
    for b in range(BR_DEV):
        first = start[tok * BR_DEV + b]
        covers = (first <= pos) & (pos < first + length[tok * BR_DEV + b])
        alive = alive | covers
        opening = opening | (covers & (first == pos))
    return alive, opening, parent[tok * BR_DEV, 0] >= 0


def tail_of(tok, start, parent):
    row = tok * BR_DEV
    token = start[jnp.maximum(parent[row, 0], 0)] + parent[row, 1]
    return lax.shift_right_logical(token, 10), lax.shift_right_logical(token, 7) & (GROUP - 1)


def send(src, dst, sems, slot, tok, head):
    copy = pltpu.make_async_remote_copy(
        src_ref=src,
        dst_ref=dst,
        send_sem=sems.at[0, slot],
        recv_sem=sems.at[1, slot],
        device_id=(tok, head),
        device_id_type=MESH,
    )
    copy.start()
    return copy


def meet(partners):
    barrier = pltpu.get_barrier_semaphore()
    for tok, head in partners:
        pl.semaphore_signal(barrier, inc=1, device_id=(tok, head), device_id_type=MESH)
    pl.semaphore_wait(barrier, len(partners))


def wrap(value, count):
    return lax.rem(value + count, count)


def fetch_kernel(
    start, length, parent, sink, key, value, prev, sinks,
    pair, a_buf, near, b_send, b_recv, mine, tail, tile, table,
    a_sems, s_sems, n_sems, b_sems, c_sems,
):
    tok, head = place()
    peers = [(tok, wrap(head + t, GROUP)) for t in range(1, GROUP)]
    later = [(wrap(tok + s, RING), head) for s in range(1, LAG + 1)]
    earlier = [(wrap(tok - s, RING), head) for s in range(1, LAG + 1)]
    meet(peers + later + earlier)

    pair[:, :, :KV] = key[...].reshape(GROUP, ROWS, KV)
    pair[:, :, KV:] = value[...].reshape(GROUP, ROWS, KV)
    row = lax.broadcasted_iota(jnp.int32, (8, 128), 0)
    sink_tile = jnp.zeros((8, 128), F32)
    for g in range(8):
        sink_tile = jnp.where(row == g, sink[g], sink_tile)
    tile[...] = sink_tile
    copies = []
    for t, (pt, ph) in enumerate(peers, 1):
        copies.append(send(pair.at[ph], a_buf.at[t], a_sems, t, pt, ph))
    near_copy = send(pair, near, n_sems, 0, tok, wrap(head + 1, GROUP))
    sink_copies = []
    for t, (pt, ph) in enumerate(peers, 1):
        sink_copies.append(send(tile, table.at[head], s_sems, t, pt, ph))
    table[head] = sink_tile
    a_buf[0] = pair[head]
    for copy in copies:
        copy.wait_recv()

    b_copies = []
    for s, (pt, ph) in enumerate(later, 1):
        _, local = tail_of(pt, start, parent)
        b_send[s - 1] = a_buf[(head - local) & (GROUP - 1)]
        b_copies.append(send(b_send.at[s - 1], b_recv.at[s - 1], b_sems, s - 1, pt, ph))
    owner, _ = tail_of(tok, start, parent)
    for copy in b_copies:
        copy.wait_recv()
    mine[...] = b_recv[jnp.clip(tok - owner - 1, 0, LAG - 1)]
    c_copies = []
    for t, (pt, ph) in enumerate(peers, 1):
        c_copies.append(send(mine, tail.at[head], c_sems, t, pt, ph))
    tail[head] = mine[...]
    alive, opening, rooted = block_state(tok, head, start, length, parent)
    ok = alive & (jnp.logical_not(opening) | rooted)
    near_copy.wait_recv()
    for copy in sink_copies:
        copy.wait_recv()
    sinks[...] = table[...].reshape(64, 128)
    for copy in c_copies:
        copy.wait_recv()
    chosen = jnp.where(opening, tail[...], near[...])
    prev[...] = jnp.where(ok, chosen, jnp.zeros_like(chosen)).reshape(WINDOW, 2 * KV)
    for copy in copies + [near_copy] + sink_copies + b_copies + c_copies:
        copy.wait_send()


def dot(left, right, dims):
    return lax.dot_general(left, right, (dims, ((), ())), preferred_element_type=F32)


def both_sides(block, lo):
    turned = pltpu.roll(block, HEAD_DIM, 1)
    zero = jnp.zeros_like(block)
    return (
        (jnp.where(lo, block, zero), jnp.where(lo, zero, turned)),
        (jnp.where(lo, turned, zero), jnp.where(lo, zero, block)),
    )


def join_sides(parts, lo):
    (a0, a1), (b0, b1) = parts
    return jnp.where(lo, a0, b1) + pltpu.roll(jnp.where(lo, b0, a1), HEAD_DIM, 1)


def attend_kernel(
    start, length, parent, query, grad, key, value, prev_key, prev_value, sinks,
    out, query_grad, own_k, own_v, prev_k, prev_v, sink_part,
):
    tok, head = place()
    alive, opening, rooted = block_state(tok, head, start, length, parent)
    ok = alive & (jnp.logical_not(opening) | rooted)
    lo = lax.broadcasted_iota(jnp.int32, (WINDOW, 128), 1) < HEAD_DIM
    place_j = lax.broadcasted_iota(jnp.int32, (WINDOW, 256), 0)
    place_i = lax.broadcasted_iota(jnp.int32, (WINDOW, 256), 1) & (WINDOW - 1)
    causal = place_j <= place_i
    bias = jnp.where(ok, 0.0, -jnp.inf)
    k_own = both_sides(key[...].astype(F32) * 0.125, lo)
    k_prev = both_sides(prev_key[...].astype(F32) * 0.125, lo)
    v_own = both_sides(value[...].astype(F32), lo)
    v_prev = both_sides(prev_value[...].astype(F32), lo)
    zero16 = jnp.zeros((WINDOW, 256), BF16)
    dks, dvs = [], []
    for c in range(2):
        k32 = [jnp.concatenate([k_own[c][e], k_prev[c][e]], 0) for e in range(2)]
        v32 = [jnp.concatenate([v_own[c][e], v_prev[c][e]], 0) for e in range(2)]
        k16 = [k.astype(BF16) for k in k32]
        v16 = [v.astype(BF16) for v in v32]
        k_turned = jnp.concatenate(k32, 0).T.astype(BF16)
        v_turned = jnp.concatenate(v32, 0).T.astype(BF16)
        dk = [jnp.zeros((256, 128), F32)] * 2
        dv = [jnp.zeros((256, 128), F32)] * 2
        for half in range(2):
            lanes = [512 * c + 256 * half + 128 * q for q in range(2)]
            q_rows = jnp.concatenate([query[:, at : at + 128] for at in lanes], 0)
            g_rows = jnp.concatenate([grad[:, at : at + 128] for at in lanes], 0)
            g_rows = jnp.where(alive, g_rows, jnp.zeros_like(g_rows))
            probs, slopes = [], []
            for e in range(2):
                heads = [8 * c + 4 * half + 2 * q + e for q in range(2)]
                scores = dot(k16[e], q_rows, ((1,), (1,)))
                scores = jnp.where(causal, scores[:WINDOW], scores[WINDOW:] + bias)
                inner = dot(v16[e], g_rows, ((1,), (1,)))
                inner = jnp.where(causal, inner[:WINDOW], inner[WINDOW:])
                sink = jnp.concatenate([sinks[h : h + 1, :] for h in heads], 1)
                peak = jnp.maximum(jnp.max(scores, axis=0, keepdims=True), sink)
                exps = jnp.exp(scores - peak)
                sink_exp = jnp.exp(sink - peak)
                inverse = 1.0 / (jnp.sum(exps, axis=0, keepdims=True) + sink_exp)
                prob = exps * inverse
                weighed = prob * inner
                delta = jnp.sum(weighed, axis=0, keepdims=True)
                slope = weighed - prob * delta
                term = sink_exp * inverse * delta
                for q, h in enumerate(heads):
                    sink_part[h : h + 1, :] = term[:, 128 * q : 128 * q + 128]
                prob16 = prob.astype(BF16)
                slope16 = slope.astype(BF16)
                prob2 = jnp.concatenate(
                    [jnp.where(causal, prob16, zero16), jnp.where(causal, zero16, prob16)], 0
                )
                slope2 = jnp.concatenate(
                    [jnp.where(causal, slope16, zero16), jnp.where(causal, zero16, slope16)], 0
                )
                dk[e] = dk[e] + dot(slope2, q_rows, ((1,), (0,)))
                dv[e] = dv[e] + dot(prob2, g_rows, ((1,), (0,)))
                probs.append(prob2)
                slopes.append(slope2)
            blended = dot(v_turned, jnp.concatenate(probs, 0), ((1,), (0,)))
            blended = jnp.where(alive, blended, jnp.zeros_like(blended))
            turned = dot(k_turned, jnp.concatenate(slopes, 0), ((1,), (0,)))
            for q, at in enumerate(lanes):
                out[:, at : at + 128] = blended[:, 128 * q : 128 * q + 128].T.astype(BF16)
                query_grad[:, at : at + 128] = turned[:, 128 * q : 128 * q + 128].T.astype(BF16)
        dks.append(dk)
        dvs.append(dv)
    own_k[...] = join_sides([[d[:WINDOW] for d in dk] for dk in dks], lo) * 0.125
    own_v[...] = join_sides([[d[:WINDOW] for d in dv] for dv in dvs], lo)
    prev_k[...] = (join_sides([[d[WINDOW:] for d in dk] for dk in dks], lo) * 0.125).astype(BF16)
    prev_v[...] = join_sides([[d[WINDOW:] for d in dv] for dv in dvs], lo).astype(BF16)


def give_kernel(
    start, length, parent, own_k, own_v, prev_k, prev_v, sink_part, key_grad, value_grad, sink_grad,
    tails, d_buf, near_send, near, e_send, e_recv, f_send, f_recv, s_send, s_recv, z_send, z_recv, x_send, x_recv,
    d_sems, s_sems, n_sems, e_sems, z_sems, f_sems, x_sems,
):
    tok, head = place()
    x, z = tok // Z, lax.rem(tok, Z)
    peers = [(tok, wrap(head + t, GROUP)) for t in range(1, GROUP)]
    later = [(wrap(tok + s, RING), head) for s in range(1, LAG + 1)]
    earlier = [(wrap(tok - s, RING), head) for s in range(1, LAG + 1)]
    z_peers = [(x * Z + wrap(z + t, Z), head) for t in range(1, Z)]
    x_peers = [(wrap(x + t, X) * Z + z, head) for t in range(1, X)]
    meet(peers + later + earlier + z_peers + x_peers)
    alive, opening, rooted = block_state(tok, head, start, length, parent)
    outward = opening & rooted
    inward = alive & jnp.logical_not(opening)
    for part, ref in enumerate((prev_k, prev_v)):
        block = ref[...].reshape(GROUP, ROWS, KV)
        lanes = slice(part * KV, part * KV + KV)
        tails[:, :, lanes] = jnp.where(outward, block, jnp.zeros_like(block))
        near_send[:, :, lanes] = jnp.where(inward, block, jnp.zeros_like(block))
    s_send[...] = sink_part[...].reshape(GROUP, 8, 128)
    copies, sink_copies = [], []
    for t, (pt, ph) in enumerate(peers, 1):
        copies.append(send(tails.at[ph], d_buf.at[t], d_sems, t, pt, ph))
    for t, (pt, ph) in enumerate(peers, 1):
        sink_copies.append(send(s_send.at[ph], s_recv.at[t], s_sems, t, pt, ph))
    near_copy = send(near_send, near, n_sems, 0, tok, wrap(head - 1, GROUP))
    total = tails[head].astype(F32)
    for t, copy in enumerate(copies, 1):
        copy.wait_recv()
        total = total + d_buf[t].astype(F32)
    owner, _ = tail_of(tok, start, parent)
    e_copies = []
    for s, (pt, ph) in enumerate(earlier, 1):
        e_send[s - 1] = jnp.where(tok - owner == s, total, jnp.zeros_like(total)).astype(BF16)
        e_copies.append(send(e_send.at[s - 1], e_recv.at[s - 1], e_sems, s - 1, pt, ph))
    sink_sum = s_send[head]
    for t, copy in enumerate(sink_copies, 1):
        copy.wait_recv()
        sink_sum = sink_sum + s_recv[t]
    z_send[...] = sink_sum
    z_copies = []
    for t, (pt, ph) in enumerate(z_peers, 1):
        z_copies.append(send(z_send, z_recv.at[t], z_sems, t, pt, ph))
    for copy in e_copies:
        copy.wait_recv()
    locals_ = [tail_of(pt, start, parent)[1] for pt, _ in later]
    arrived = [e_recv[s].astype(F32) for s in range(LAG)]
    f_copies = []

    def landed(place_):
        landing = jnp.zeros((ROWS, 2 * KV), F32)
        for s in range(LAG):
            landing = landing + jnp.where(locals_[s] == place_, arrived[s], 0.0)
        return landing.astype(BF16)

    for t, (pt, ph) in enumerate(peers, 1):
        f_send[t] = landed(ph)
        f_copies.append(send(f_send.at[t], f_recv.at[head], f_sems, t, pt, ph))
    f_recv[head] = landed(head)
    for t, copy in enumerate(z_copies, 1):
        copy.wait_recv()
        sink_sum = sink_sum + z_recv[t]
    x_send[...] = sink_sum
    x_copies = []
    for t, (pt, ph) in enumerate(x_peers, 1):
        x_copies.append(send(x_send, x_recv.at[t], x_sems, t, pt, ph))
    near_copy.wait_recv()
    for copy in f_copies:
        copy.wait_recv()
    back = f_recv[...].astype(F32) + near[...].astype(F32)
    back = back.reshape(WINDOW, 2 * KV)
    key_grad[...] = (own_k[...] + back[:, :KV]).astype(BF16)
    value_grad[...] = (own_v[...] + back[:, KV:]).astype(BF16)
    for t, copy in enumerate(x_copies, 1):
        copy.wait_recv()
        sink_sum = sink_sum + x_recv[t]
    sums = jnp.sum(sink_sum, axis=1, keepdims=True)
    row = lax.broadcasted_iota(jnp.int32, (8, 128), 0)
    lane = lax.broadcasted_iota(jnp.int32, (8, 128), 1)
    line = jnp.sum(jnp.where(row == lane, sums, 0.0), axis=0)
    sink_grad[...] = -line[:8]
    for copy in copies + sink_copies + [near_copy] + e_copies + z_copies + f_copies + x_copies:
        copy.wait_send()


SMEM = pl.BlockSpec(memory_space=pltpu.SMEM)
VMEM = pl.BlockSpec(memory_space=pltpu.VMEM)
DMA = pltpu.SemaphoreType.DMA


def local(queries, key_states, value_states, out_grad, sink_logits, branch_start, branch_len, parent_list):
    slices = (GROUP, ROWS, 2 * KV)
    one = (ROWS, 2 * KV)
    prev, sinks = pl.pallas_call(
        fetch_kernel,
        name="fetch",
        out_shape=(
            jax.ShapeDtypeStruct((WINDOW, 2 * KV), BF16),
            jax.ShapeDtypeStruct((64, 128), F32),
        ),
        in_specs=[SMEM] * 4 + [VMEM] * 2,
        out_specs=(VMEM, VMEM),
        scratch_shapes=[
            pltpu.VMEM(slices, BF16),
            pltpu.VMEM(slices, BF16),
            pltpu.VMEM(slices, BF16),
            pltpu.VMEM((LAG,) + one, BF16),
            pltpu.VMEM((LAG,) + one, BF16),
            pltpu.VMEM(one, BF16),
            pltpu.VMEM(slices, BF16),
            pltpu.VMEM((8, 128), F32),
            pltpu.VMEM((GROUP, 8, 128), F32),
            DMA((2, GROUP)),
            DMA((2, GROUP)),
            DMA((2, 1)),
            DMA((2, LAG)),
            DMA((2, GROUP)),
        ],
        compiler_params=pltpu.CompilerParams(collective_id=0, has_side_effects=True),
    )(branch_start, branch_len, parent_list, sink_logits, key_states, value_states)

    wide = pl.BlockSpec((WINDOW, 1024), lambda p: (0, p))
    narrow = pl.BlockSpec((WINDOW, 128), lambda p: (0, p))
    narrow_v = pl.BlockSpec((WINDOW, 128), lambda p: (0, p + 4))
    lines = pl.BlockSpec((16, 128), lambda p: (p, 0))
    attn_out, query_grad, own_k, own_v, prev_k, prev_v, sink_part = pl.pallas_call(
        attend_kernel,
        name="attend",
        grid=(4,),
        out_shape=(
            jax.ShapeDtypeStruct((WINDOW, 4096), BF16),
            jax.ShapeDtypeStruct((WINDOW, 4096), BF16),
            jax.ShapeDtypeStruct((WINDOW, KV), F32),
            jax.ShapeDtypeStruct((WINDOW, KV), F32),
            jax.ShapeDtypeStruct((WINDOW, KV), BF16),
            jax.ShapeDtypeStruct((WINDOW, KV), BF16),
            jax.ShapeDtypeStruct((64, 128), F32),
        ),
        in_specs=[SMEM] * 3 + [wide, wide, narrow, narrow, narrow, narrow_v, lines],
        out_specs=(wide, wide, narrow, narrow, narrow, narrow, lines),
        compiler_params=pltpu.CompilerParams(vmem_limit_bytes=48 * 1024 * 1024),
    )(branch_start, branch_len, parent_list, queries, out_grad, key_states, value_states, prev, prev, sinks)

    key_grad, value_grad, sink_grad = pl.pallas_call(
        give_kernel,
        name="give",
        out_shape=(
            jax.ShapeDtypeStruct((WINDOW, KV), BF16),
            jax.ShapeDtypeStruct((WINDOW, KV), BF16),
            jax.ShapeDtypeStruct((8,), F32),
        ),
        in_specs=[SMEM] * 3 + [VMEM] * 5,
        out_specs=(VMEM, VMEM, VMEM),
        scratch_shapes=[
            pltpu.VMEM(slices, BF16),
            pltpu.VMEM(slices, BF16),
            pltpu.VMEM(slices, BF16),
            pltpu.VMEM(slices, BF16),
            pltpu.VMEM((LAG,) + one, BF16),
            pltpu.VMEM((LAG,) + one, BF16),
            pltpu.VMEM(slices, BF16),
            pltpu.VMEM(slices, BF16),
            pltpu.VMEM((GROUP, 8, 128), F32),
            pltpu.VMEM((GROUP, 8, 128), F32),
            pltpu.VMEM((8, 128), F32),
            pltpu.VMEM((Z, 8, 128), F32),
            pltpu.VMEM((8, 128), F32),
            pltpu.VMEM((X, 8, 128), F32),
            DMA((2, GROUP)),
            DMA((2, GROUP)),
            DMA((2, 1)),
            DMA((2, LAG)),
            DMA((2, Z)),
            DMA((2, GROUP)),
            DMA((2, X)),
        ],
        compiler_params=pltpu.CompilerParams(collective_id=1, has_side_effects=True),
    )(branch_start, branch_len, parent_list, own_k, own_v, prev_k, prev_v, sink_part)
    return attn_out, query_grad, key_grad, value_grad, sink_grad


def solution(mesh):
    rows = P(("tok", "head"), None)
    return jax.shard_map(
        local,
        mesh=mesh,
        in_specs=(rows, rows, rows, rows, P("head"), P(), P(), P()),
        out_specs=(rows, rows, rows, rows, P("head")),
        check_vma=False,
    )
```

```python
import jax
import jax.numpy as jnp
from jax import lax
from jax.experimental import pallas as pl
from jax.experimental.pallas import tpu as pltpu
from jax.sharding import PartitionSpec as P

HEAD_DIM = 64
WINDOW = 128
LAG = 3
PAIRS = 4
BR_DEV = 2
GROUP = 8
RING = 32
ROWS = WINDOW // GROUP
KV = 512
Z = 8
X = 4
F32 = jnp.float32
BF16 = jnp.bfloat16
MESH = pl.DeviceIdType.MESH


def place():
    return lax.axis_index("tok"), lax.axis_index("head")


def block_state(tok, head, start, length, parent):
    pos = (tok * GROUP + head) * WINDOW
    alive, opening = False, False
    for b in range(BR_DEV):
        first = start[tok * BR_DEV + b]
        covers = (first <= pos) & (pos < first + length[tok * BR_DEV + b])
        alive = alive | covers
        opening = opening | (covers & (first == pos))
    return alive, opening, parent[0, tok * BR_DEV] >= 0


def tail_of(tok, start, parent):
    row = tok * BR_DEV
    token = start[jnp.maximum(parent[0, row], 0)] + parent[1, row]
    return lax.shift_right_logical(token, 10), lax.shift_right_logical(token, 7) & (GROUP - 1)


def send(src, dst, sems, slot, tok, head):
    copy = pltpu.make_async_remote_copy(
        src_ref=src,
        dst_ref=dst,
        send_sem=sems.at[0, slot],
        recv_sem=sems.at[1, slot],
        device_id=(tok, head),
        device_id_type=MESH,
    )
    copy.start()
    return copy


def wrap(value, count):
    return lax.rem(value + count, count)


def dot(left, right, dims):
    return lax.dot_general(left, right, (dims, ((), ())), preferred_element_type=F32)


def both_sides(block, lo):
    turned = pltpu.roll(block, HEAD_DIM, 1)
    zero = jnp.zeros_like(block)
    return (
        (jnp.where(lo, block, zero), jnp.where(lo, zero, turned)),
        (jnp.where(lo, turned, zero), jnp.where(lo, zero, block)),
    )


def join_sides(parts, lo):
    (a0, a1), (b0, b1) = parts
    return jnp.where(lo, a0, b1) + pltpu.roll(jnp.where(lo, b0, a1), HEAD_DIM, 1)


FAR_FIRST = (4, 5, 3, 6, 2, 7, 1)


def split_rows(rows):
    high = rows.astype(BF16).astype(F32)
    return jnp.concatenate([high, rows - high], 1).astype(BF16)


def kernel(
    start, length, parent, sink, queries, out_grad, keys, values,
    attn_out, query_grad, key_grad, value_grad, sink_grad,
    query, grad, out, turned_out, pair, a_buf, near, b_send, b_recv, mine, tail, prev, table,
    s_own, p_own, probs, slopes, own_k, own_v,
    give, d_buf, near_send, near_back, e_send, e_recv, f_send, f_recv, z_send, z_recv, x_send, x_recv, part,
    load_sems, store_sems, a_sems, n_sems, b_sems, c_sems, d_sems, e_sems, f_sems, z_sems, x_sems,
):
    tok, head = place()
    x, z = tok // Z, lax.rem(tok, Z)
    peers = [(t, (tok, wrap(head + t, GROUP))) for t in FAR_FIRST]
    later = [(s, (wrap(tok + s, RING), head)) for s in (3, 2, 1)]
    earlier = [(s, (wrap(tok - s, RING), head)) for s in (3, 2, 1)]
    z_peers = [(t, (x * Z + wrap(z + t, Z), head)) for t in FAR_FIRST]
    x_peers = [(t, (wrap(x + t, X) * Z + z, head)) for t in (2, 3, 1)]
    right, left = (tok, wrap(head + 1, GROUP)), (tok, wrap(head - 1, GROUP))

    loads = [
        pltpu.make_async_copy(src, dst, load_sems.at[n])
        for n, (src, dst) in enumerate((
            (keys, pair.at[:, pl.ds(0, KV)]), (values, pair.at[:, pl.ds(KV, KV)]), (queries, query), (out_grad, grad),
        ))
    ]
    for load in loads:
        load.start()
    barrier = pltpu.get_barrier_semaphore()
    partners = [who for _, who in z_peers + later + earlier + peers + x_peers]
    for who in partners:
        pl.semaphore_signal(barrier, inc=1, device_id=who, device_id_type=MESH)

    alive, opening, rooted = block_state(tok, head, start, length, parent)
    ok = alive & (jnp.logical_not(opening) | rooted)
    outward = opening & rooted
    inward = alive & jnp.logical_not(opening)
    row = lax.broadcasted_iota(jnp.int32, (8, 128), 0)
    lane = lax.broadcasted_iota(jnp.int32, (8, 128), 1)
    sink_tile = jnp.zeros((8, 128), F32)
    for g in range(8):
        sink_tile = jnp.where(row == g, sink[g], sink_tile)
    table[head] = sink_tile
    pair[:, 2 * KV :] = split_rows(jnp.broadcast_to(sink_tile[None], (GROUP, 8, 128))).reshape(WINDOW, 128)
    loads[0].wait()
    loads[1].wait()
    pl.semaphore_wait(barrier, len(partners))

    def rows_of(place_):
        return pl.ds(pl.multiple_of(place_ * ROWS, ROWS), ROWS)

    sent = []

    def ship(src, dst, sems, slot, who):
        copy = send(src, dst, sems, slot, *who)
        sent.append(copy)
        return copy

    a_copies = [(t, ship(pair.at[rows_of(who[1])], a_buf.at[t], a_sems, t, who)) for t, who in peers]
    near_copy = ship(pair.at[:, pl.ds(0, 2 * KV)], near, n_sems, 0, right)
    a_buf[0] = pair[rows_of(head), :]

    lo = lax.broadcasted_iota(jnp.int32, (WINDOW, 128), 1) < HEAD_DIM
    place_j = lax.broadcasted_iota(jnp.int32, (WINDOW, 256), 0)
    place_i = lax.broadcasted_iota(jnp.int32, (WINDOW, 256), 1) & (WINDOW - 1)
    causal = place_j <= place_i
    causal16 = causal.astype(F32).astype(BF16)
    bias = jnp.where(ok, 0.0, -jnp.inf)

    def lanes_at(at, size=128):
        return pl.ds(pl.multiple_of(at, size), size)

    def sides(ref, p, factor):
        k = both_sides(ref[:, lanes_at(p * 128)].astype(F32) * factor, lo)
        v = both_sides(ref[:, lanes_at(KV + p * 128)].astype(F32), lo)
        return k, v

    def stacked(ref, at):
        return jnp.concatenate([ref[:, lanes_at(at)], ref[:, lanes_at(at + 128)]], 0)

    def before(p, carry):
        wide = lanes_at(p * 1024, 1024)
        grad[:, wide] = jnp.where(alive, grad[:, wide], jnp.zeros((), BF16))
        k, v = sides(pair, p, 0.125)
        for c in range(2):
            for half in range(2):
                at = p * 1024 + 512 * c + 256 * half
                q_rows, g_rows = stacked(query, at), stacked(grad, at)
                for e in range(2):
                    unit = 4 * c + 2 * half + e
                    s_own[p, unit] = dot(k[c][e].astype(BF16), q_rows, ((1,), (1,)))
                    p_own[p, unit] = dot(v[c][e].astype(BF16), g_rows, ((1,), (1,)))
        return carry

    loads[2].wait()
    loads[3].wait()
    lax.fori_loop(0, PAIRS, before, 0)

    for t, copy in a_copies:
        copy.wait_recv()
    b_copies = []
    for s, who in later:
        _, place_ = tail_of(who[0], start, parent)
        b_send[s - 1] = a_buf[(head - place_) & (GROUP - 1)][:, : 2 * KV]
        b_copies.append(ship(b_send.at[s - 1], b_recv.at[s - 1], b_sems, s - 1, who))
    for t in range(1, GROUP):
        extra = a_buf[t, :, 2 * KV :].astype(F32)
        table[wrap(head - t, GROUP)] = extra[:8] + extra[8:]
    owner, _ = tail_of(tok, start, parent)
    for copy in b_copies:
        copy.wait_recv()
    mine[...] = b_recv[jnp.clip(tok - owner - 1, 0, LAG - 1)]
    c_copies = [ship(mine, tail.at[rows_of(head)], c_sems, t, who) for t, who in peers]
    tail[rows_of(head), :] = mine[...]
    near_copy.wait_recv()
    for copy in c_copies:
        copy.wait_recv()
    prev[...] = jnp.where(ok, jnp.where(opening, tail[...], near[...]), jnp.zeros((), BF16))

    def during(p, carry):
        k, v = sides(prev, p, 0.125)
        dks, dvs = [], []
        for c in range(2):
            dk = [jnp.zeros((WINDOW, 128), F32)] * 2
            dv = [jnp.zeros((WINDOW, 128), F32)] * 2
            for half in range(2):
                at = p * 1024 + 512 * c + 256 * half
                q_rows, g_rows = stacked(query, at), stacked(grad, at)
                for e in range(2):
                    unit = 4 * c + 2 * half + e
                    lines = [4 * half + 2 * q + e for q in range(2)]
                    scores = dot(k[c][e].astype(BF16), q_rows, ((1,), (1,)))
                    scores = jnp.where(causal, s_own[p, unit], scores + bias)
                    inner = dot(v[c][e].astype(BF16), g_rows, ((1,), (1,)))
                    inner = jnp.where(causal, p_own[p, unit], inner)
                    sinks = jnp.concatenate([table[2 * p + c, h : h + 1, :] for h in lines], 1)
                    peak = jnp.maximum(jnp.max(scores, axis=0, keepdims=True), sinks)
                    exps = jnp.exp(scores - peak)
                    sink_exp = jnp.exp(sinks - peak)
                    inverse = 1.0 / (jnp.sum(exps, axis=0, keepdims=True) + sink_exp)
                    prob = exps * inverse
                    weighed = prob * inner
                    delta = jnp.sum(weighed, axis=0, keepdims=True)
                    slope = weighed - prob * delta
                    term = sink_exp * inverse * delta
                    for q, h in enumerate(lines):
                        part[2 * p + c, h : h + 1, :] = term[:, 128 * q : 128 * q + 128]
                    prob16 = prob.astype(BF16)
                    slope16 = slope.astype(BF16)
                    probs[p, unit] = prob16
                    slopes[p, unit] = slope16
                    dk[e] = dk[e] + dot(slope16 - slope16 * causal16, q_rows, ((1,), (0,)))
                    dv[e] = dv[e] + dot(prob16 - prob16 * causal16, g_rows, ((1,), (0,)))
            dks.append(dk)
            dvs.append(dv)
        zero16 = jnp.zeros((), BF16)
        for at, block in ((p * 128, join_sides(dks, lo) * 0.125), (KV + p * 128, join_sides(dvs, lo))):
            block = block.astype(BF16)
            give[:, lanes_at(at)] = jnp.where(outward, block, zero16)
            near_send[:, lanes_at(at)] = jnp.where(inward, block, zero16)
        return carry

    lax.fori_loop(0, PAIRS, during, 0)
    give[:, 2 * KV :] = split_rows(part[...]).reshape(WINDOW, 128)

    d_copies = [(t, ship(give.at[rows_of(who[1])], d_buf.at[t], d_sems, t, who)) for t, who in peers]
    back_copy = ship(near_send, near_back, n_sems, 1, left)

    def stores(p):
        wide = lanes_at(p * 1024, 1024)
        return (
            pltpu.make_async_copy(out.at[:, wide], attn_out.at[:, wide], store_sems.at[0, p]),
            pltpu.make_async_copy(turned_out.at[:, wide], query_grad.at[:, wide], store_sems.at[1, p]),
        )

    def after(p, carry):
        k_own, v_own = sides(pair, p, 0.125)
        k_prev, v_prev = sides(prev, p, 0.125)
        dks, dvs = [], []
        for c in range(2):
            k_all = jnp.concatenate([k_own[c][0], k_prev[c][0], k_own[c][1], k_prev[c][1]], 0)
            v_all = jnp.concatenate([v_own[c][0], v_prev[c][0], v_own[c][1], v_prev[c][1]], 0)
            k_turned = k_all.T.astype(BF16)
            v_turned = v_all.T.astype(BF16)
            dk = [jnp.zeros((WINDOW, 128), F32)] * 2
            dv = [jnp.zeros((WINDOW, 128), F32)] * 2
            for half in range(2):
                at = p * 1024 + 512 * c + 256 * half
                q_rows, g_rows = stacked(query, at), stacked(grad, at)
                prob_all, slope_all = [], []
                for e in range(2):
                    unit = 4 * c + 2 * half + e
                    prob16, slope16 = probs[p, unit], slopes[p, unit]
                    prob_own, slope_own = prob16 * causal16, slope16 * causal16
                    dk[e] = dk[e] + dot(slope_own, q_rows, ((1,), (0,)))
                    dv[e] = dv[e] + dot(prob_own, g_rows, ((1,), (0,)))
                    prob_all += [prob_own, prob16 - prob_own]
                    slope_all += [slope_own, slope16 - slope_own]
                blended = dot(v_turned, jnp.concatenate(prob_all, 0), ((1,), (0,)))
                blended = jnp.where(alive, blended, 0.0)
                turned = dot(k_turned, jnp.concatenate(slope_all, 0), ((1,), (0,)))
                for q in range(2):
                    piece = slice(128 * q, 128 * q + 128)
                    out[:, lanes_at(at + 128 * q)] = blended[:, piece].T.astype(BF16)
                    turned_out[:, lanes_at(at + 128 * q)] = turned[:, piece].T.astype(BF16)
            dks.append(dk)
            dvs.append(dv)
        own_k[:, lanes_at(p * 128)] = join_sides(dks, lo) * 0.125
        own_v[:, lanes_at(p * 128)] = join_sides(dvs, lo)
        return carry

    lax.fori_loop(0, PAIRS // 2, after, 0)
    total = give[rows_of(head), :].astype(F32)
    for t, copy in d_copies:
        copy.wait_recv()
        total = total + d_buf[t].astype(F32)
    slices = total[:, : 2 * KV]
    e_copies = []
    for s, who in earlier:
        e_send[s - 1] = jnp.where(tok - owner == s, slices, 0.0).astype(BF16)
        e_copies.append(ship(e_send.at[s - 1], e_recv.at[s - 1], e_sems, s - 1, who))
    sink_sum = total[:8, 2 * KV :] + total[8:, 2 * KV :]
    z_send[...] = sink_sum
    z_copies = [(t, ship(z_send, z_recv.at[t], z_sems, t, who)) for t, who in z_peers]
    for p in range(PAIRS // 2):
        for store in stores(p):
            store.start()
    lax.fori_loop(PAIRS // 2, PAIRS, after, 0)
    for copy in e_copies:
        copy.wait_recv()
    places = [tail_of(wrap(tok + s, RING), start, parent)[1] for s in range(1, LAG + 1)]
    arrived = [e_recv[s].astype(F32) for s in range(LAG)]

    def landed(place_):
        landing = jnp.zeros((ROWS, 2 * KV), F32)
        for s in range(LAG):
            landing = landing + jnp.where(places[s] == place_, arrived[s], 0.0)
        return landing.astype(BF16)

    f_copies = []
    for t, who in peers:
        f_send[t] = landed(who[1])
        f_copies.append(ship(f_send.at[t], f_recv.at[rows_of(head)], f_sems, t, who))
    f_recv[rows_of(head), :] = landed(head)
    for p in range(PAIRS // 2, PAIRS):
        for store in stores(p):
            store.start()
    for t, copy in z_copies:
        copy.wait_recv()
        sink_sum = sink_sum + z_recv[t]
    x_send[...] = sink_sum
    x_copies = [(t, ship(x_send, x_recv.at[t], x_sems, t, who)) for t, who in x_peers]
    back_copy.wait_recv()
    own_k[...] = own_k[...] + near_back[:, :KV].astype(F32)
    own_v[...] = own_v[...] + near_back[:, KV:].astype(F32)
    for copy in f_copies:
        copy.wait_recv()
    key_grad[...] = (own_k[...] + f_recv[:, :KV].astype(F32)).astype(BF16)
    value_grad[...] = (own_v[...] + f_recv[:, KV:].astype(F32)).astype(BF16)
    for t, copy in x_copies:
        copy.wait_recv()
        sink_sum = sink_sum + x_recv[t]
    sums = jnp.sum(sink_sum, axis=1, keepdims=True)
    line = jnp.sum(jnp.where(row == lane, sums, 0.0), axis=0)
    sink_grad[...] = -line[:8]
    for copy in sent:
        copy.wait_send()
    for p in range(PAIRS):
        for store in stores(p):
            store.wait()


SMEM = pl.BlockSpec(memory_space=pltpu.SMEM)
VMEM = pl.BlockSpec(memory_space=pltpu.VMEM)
ANY = pl.BlockSpec(memory_space=pl.ANY)
DMA = pltpu.SemaphoreType.DMA


def local(queries, key_states, value_states, out_grad, sink_logits, branch_start, branch_len, parent_list):
    block = pltpu.VMEM((WINDOW, 2 * KV), BF16)
    more = 2 * KV + 128
    three = pltpu.VMEM((LAG, ROWS, 2 * KV), BF16)
    rows = pltpu.VMEM((WINDOW, 4096), BF16)
    units = (PAIRS, 8, WINDOW, 256)
    return pl.pallas_call(
        kernel,
        name="banded",
        out_shape=(
            jax.ShapeDtypeStruct((WINDOW, 4096), BF16),
            jax.ShapeDtypeStruct((WINDOW, 4096), BF16),
            jax.ShapeDtypeStruct((WINDOW, KV), BF16),
            jax.ShapeDtypeStruct((WINDOW, KV), BF16),
            jax.ShapeDtypeStruct((8,), F32),
        ),
        in_specs=[SMEM] * 4 + [ANY] * 4,
        out_specs=(ANY, ANY, VMEM, VMEM, VMEM),
        scratch_shapes=[
            rows, rows, rows, rows,
            pltpu.VMEM((WINDOW, more), BF16),
            pltpu.VMEM((GROUP, ROWS, more), BF16),
            block,
            three, three,
            pltpu.VMEM((ROWS, 2 * KV), BF16),
            block, block,
            pltpu.VMEM((GROUP, 8, 128), F32),
            pltpu.VMEM(units, F32), pltpu.VMEM(units, F32),
            pltpu.VMEM(units, BF16), pltpu.VMEM(units, BF16),
            pltpu.VMEM((WINDOW, KV), F32), pltpu.VMEM((WINDOW, KV), F32),
            pltpu.VMEM((WINDOW, more), BF16),
            pltpu.VMEM((GROUP, ROWS, more), BF16),
            block, block,
            three, three,
            pltpu.VMEM((GROUP, ROWS, 2 * KV), BF16),
            block,
            pltpu.VMEM((8, 128), F32), pltpu.VMEM((Z, 8, 128), F32),
            pltpu.VMEM((8, 128), F32), pltpu.VMEM((X, 8, 128), F32),
            pltpu.VMEM((GROUP, 8, 128), F32),
            DMA((4,)), DMA((2, PAIRS)),
            DMA((2, GROUP)), DMA((2, 2)), DMA((2, LAG)), DMA((2, GROUP)),
            DMA((2, GROUP)), DMA((2, LAG)), DMA((2, GROUP)), DMA((2, Z)), DMA((2, X)),
        ],
        compiler_params=pltpu.CompilerParams(
            collective_id=0, has_side_effects=True, vmem_limit_bytes=56 * 1024 * 1024
        ),
    )(branch_start, branch_len, parent_list.T, sink_logits, queries, out_grad, key_states, value_states)


def solution(mesh):
    rows = P(("tok", "head"), None)
    return jax.shard_map(
        local,
        mesh=mesh,
        in_specs=(rows, rows, rows, rows, P("head"), P(), P(), P()),
        out_specs=(rows, rows, rows, rows, P("head")),
        check_vma=False,
    )
```

```python
import jax
import jax.numpy as jnp
from jax import lax
from jax.experimental import pallas as pl
from jax.experimental.pallas import tpu as pltpu
from jax.sharding import PartitionSpec as P

HEAD_DIM = 64
WINDOW = 128
LAG = 3
PAIRS = 4
BR_DEV = 2
GROUP = 8
RING = 32
ROWS = WINDOW // GROUP
KV = 512
Z = 8
X = 4
F32 = jnp.float32
BF16 = jnp.bfloat16
MESH = pl.DeviceIdType.MESH


def place():
    return lax.axis_index("tok"), lax.axis_index("head")


def block_state(tok, head, start, length, parent):
    pos = (tok * GROUP + head) * WINDOW
    alive, opening = False, False
    for b in range(BR_DEV):
        first = start[tok * BR_DEV + b]
        covers = (first <= pos) & (pos < first + length[tok * BR_DEV + b])
        alive = alive | covers
        opening = opening | (covers & (first == pos))
    return alive, opening, parent[0, tok * BR_DEV] >= 0


def tail_of(tok, start, parent):
    row = tok * BR_DEV
    token = start[jnp.maximum(parent[0, row], 0)] + parent[1, row]
    return lax.shift_right_logical(token, 10), lax.shift_right_logical(token, 7) & (GROUP - 1)


def send(src, dst, sems, slot, tok, head):
    copy = pltpu.make_async_remote_copy(
        src_ref=src,
        dst_ref=dst,
        send_sem=sems.at[0, slot],
        recv_sem=sems.at[1, slot],
        device_id=(tok, head),
        device_id_type=MESH,
    )
    copy.start()
    return copy


def wrap(value, count):
    return lax.rem(value + count, count)


def dot(left, right, dims):
    return lax.dot_general(left, right, (dims, ((), ())), preferred_element_type=F32)


def both_sides(block, lo):
    turned = pltpu.roll(block, HEAD_DIM, 1)
    zero = jnp.zeros_like(block)
    return (
        (jnp.where(lo, block, zero), jnp.where(lo, zero, turned)),
        (jnp.where(lo, turned, zero), jnp.where(lo, zero, block)),
    )


def join_sides(parts, lo):
    (a0, a1), (b0, b1) = parts
    return jnp.where(lo, a0, b1) + pltpu.roll(jnp.where(lo, b0, a1), HEAD_DIM, 1)


FAR_FIRST = (4, 5, 3, 6, 2, 7, 1)


def split_rows(rows):
    high = rows.astype(BF16).astype(F32)
    return jnp.concatenate([high, rows - high], 1).astype(BF16)


def kernel(
    start, length, parent, sink, queries, out_grad, keys, values,
    attn_out, query_grad, key_grad, value_grad, sink_grad,
    query, grad, pair, a_buf, near, b_send, b_recv, mine, tail, prev, table,
    s_own, p_own, probs, slopes, own_k, own_v,
    give, d_buf, near_send, near_back, e_send, e_recv, f_send, f_recv, z_send, z_recv, x_send, x_recv, part,
    load_sems, a_sems, n_sems, b_sems, c_sems, d_sems, e_sems, f_sems, z_sems, x_sems,
):
    tok, head = place()
    x, z = tok // Z, lax.rem(tok, Z)
    peers = [(t, (tok, wrap(head + t, GROUP))) for t in FAR_FIRST]
    later = [(s, (wrap(tok + s, RING), head)) for s in (3, 2, 1)]
    earlier = [(s, (wrap(tok - s, RING), head)) for s in (3, 2, 1)]
    z_peers = [(t, (x * Z + wrap(z + t, Z), head)) for t in FAR_FIRST]
    x_peers = [(t, (wrap(x + t, X) * Z + z, head)) for t in (2, 3, 1)]
    right, left = (tok, wrap(head + 1, GROUP)), (tok, wrap(head - 1, GROUP))

    loads = [
        pltpu.make_async_copy(src, dst, load_sems.at[n])
        for n, (src, dst) in enumerate((
            (keys, pair.at[:, pl.ds(0, KV)]), (values, pair.at[:, pl.ds(KV, KV)]), (queries, query), (out_grad, grad),
        ))
    ]
    for load in loads:
        load.start()
    barrier = pltpu.get_barrier_semaphore()
    partners = [who for _, who in z_peers + later + earlier + peers + x_peers]
    for who in partners:
        pl.semaphore_signal(barrier, inc=1, device_id=who, device_id_type=MESH)

    alive, opening, rooted = block_state(tok, head, start, length, parent)
    ok = alive & (jnp.logical_not(opening) | rooted)
    outward = opening & rooted
    inward = alive & jnp.logical_not(opening)
    row = lax.broadcasted_iota(jnp.int32, (8, 128), 0)
    lane = lax.broadcasted_iota(jnp.int32, (8, 128), 1)
    sink_tile = jnp.zeros((8, 128), F32)
    for g in range(8):
        sink_tile = jnp.where(row == g, sink[g], sink_tile)
    table[head] = sink_tile
    pair[:, 2 * KV :] = split_rows(jnp.broadcast_to(sink_tile[None], (GROUP, 8, 128))).reshape(WINDOW, 128)
    loads[0].wait()
    loads[1].wait()
    pl.semaphore_wait(barrier, len(partners))

    def rows_of(place_):
        return pl.ds(pl.multiple_of(place_ * ROWS, ROWS), ROWS)

    sent = []

    def ship(src, dst, sems, slot, who):
        copy = send(src, dst, sems, slot, *who)
        sent.append(copy)
        return copy

    a_copies = [(t, ship(pair.at[rows_of(who[1])], a_buf.at[t], a_sems, t, who)) for t, who in peers]
    near_copy = ship(pair.at[:, pl.ds(0, 2 * KV)], near, n_sems, 0, right)
    a_buf[0] = pair[rows_of(head), :]

    lo = lax.broadcasted_iota(jnp.int32, (WINDOW, 128), 1) < HEAD_DIM
    place_j = lax.broadcasted_iota(jnp.int32, (WINDOW, 256), 0)
    place_i = lax.broadcasted_iota(jnp.int32, (WINDOW, 256), 1) & (WINDOW - 1)
    causal = place_j <= place_i
    causal16 = causal.astype(F32).astype(BF16)
    bias = jnp.where(ok, 0.0, -jnp.inf)

    def lanes_at(at, size=128):
        return pl.ds(pl.multiple_of(at, size), size)

    def sides(ref, p, factor):
        k = both_sides(ref[:, lanes_at(p * 128)].astype(F32) * factor, lo)
        v = both_sides(ref[:, lanes_at(KV + p * 128)].astype(F32), lo)
        return k, v

    def stacked(ref, at):
        return jnp.concatenate([ref[:, lanes_at(at)], ref[:, lanes_at(at + 128)]], 0)

    def before(p, carry):
        wide = lanes_at(p * 1024, 1024)
        grad[:, wide] = jnp.where(alive, grad[:, wide], jnp.zeros((), BF16))
        k, v = sides(pair, p, 0.125)
        for c in range(2):
            for half in range(2):
                at = p * 1024 + 512 * c + 256 * half
                q_rows, g_rows = stacked(query, at), stacked(grad, at)
                for e in range(2):
                    unit = 4 * c + 2 * half + e
                    s_own[p, unit] = dot(k[c][e].astype(BF16), q_rows, ((1,), (1,)))
                    p_own[p, unit] = dot(v[c][e].astype(BF16), g_rows, ((1,), (1,)))
        return carry

    loads[2].wait()
    loads[3].wait()
    lax.fori_loop(0, PAIRS, before, 0)

    for t, copy in a_copies:
        copy.wait_recv()
    b_copies = []
    for s, who in later:
        _, place_ = tail_of(who[0], start, parent)
        b_send[s - 1] = a_buf[(head - place_) & (GROUP - 1)][:, : 2 * KV]
        b_copies.append(ship(b_send.at[s - 1], b_recv.at[s - 1], b_sems, s - 1, who))
    for t in range(1, GROUP):
        extra = a_buf[t, :, 2 * KV :].astype(F32)
        table[wrap(head - t, GROUP)] = extra[:8] + extra[8:]
    owner, _ = tail_of(tok, start, parent)
    for copy in b_copies:
        copy.wait_recv()
    mine[...] = b_recv[jnp.clip(tok - owner - 1, 0, LAG - 1)]
    c_copies = [ship(mine, tail.at[rows_of(head)], c_sems, t, who) for t, who in peers]
    tail[rows_of(head), :] = mine[...]
    near_copy.wait_recv()
    for copy in c_copies:
        copy.wait_recv()
    prev[...] = jnp.where(ok, jnp.where(opening, tail[...], near[...]), jnp.zeros((), BF16))

    def during(p, carry):
        k, v = sides(prev, p, 0.125)
        dks, dvs = [], []
        for c in range(2):
            dk = [jnp.zeros((WINDOW, 128), F32)] * 2
            dv = [jnp.zeros((WINDOW, 128), F32)] * 2
            for half in range(2):
                at = p * 1024 + 512 * c + 256 * half
                q_rows, g_rows = stacked(query, at), stacked(grad, at)
                for e in range(2):
                    unit = 4 * c + 2 * half + e
                    lines = [4 * half + 2 * q + e for q in range(2)]
                    scores = dot(k[c][e].astype(BF16), q_rows, ((1,), (1,)))
                    scores = jnp.where(causal, s_own[p, unit], scores + bias)
                    inner = dot(v[c][e].astype(BF16), g_rows, ((1,), (1,)))
                    inner = jnp.where(causal, p_own[p, unit], inner)
                    sinks = jnp.concatenate([table[2 * p + c, h : h + 1, :] for h in lines], 1)
                    peak = jnp.maximum(jnp.max(scores, axis=0, keepdims=True), sinks)
                    exps = jnp.exp(scores - peak)
                    sink_exp = jnp.exp(sinks - peak)
                    inverse = 1.0 / (jnp.sum(exps, axis=0, keepdims=True) + sink_exp)
                    prob = exps * inverse
                    weighed = prob * inner
                    delta = jnp.sum(weighed, axis=0, keepdims=True)
                    slope = weighed - prob * delta
                    term = sink_exp * inverse * delta
                    for q, h in enumerate(lines):
                        part[2 * p + c, h : h + 1, :] = term[:, 128 * q : 128 * q + 128]
                    prob16 = prob.astype(BF16)
                    slope16 = slope.astype(BF16)
                    probs[p, unit] = prob16
                    slopes[p, unit] = slope16
                    dk[e] = dk[e] + dot(slope16 - slope16 * causal16, q_rows, ((1,), (0,)))
                    dv[e] = dv[e] + dot(prob16 - prob16 * causal16, g_rows, ((1,), (0,)))
            dks.append(dk)
            dvs.append(dv)
        zero16 = jnp.zeros((), BF16)
        for at, block in ((p * 128, join_sides(dks, lo) * 0.125), (KV + p * 128, join_sides(dvs, lo))):
            block = block.astype(BF16)
            give[:, lanes_at(at)] = jnp.where(outward, block, zero16)
            near_send[:, lanes_at(at)] = jnp.where(inward, block, zero16)
        return carry

    lax.fori_loop(0, PAIRS, during, 0)
    give[:, 2 * KV :] = split_rows(part[...]).reshape(WINDOW, 128)

    d_copies = [(t, ship(give.at[rows_of(who[1])], d_buf.at[t], d_sems, t, who)) for t, who in peers]
    back_copy = ship(near_send, near_back, n_sems, 1, left)

    def after(p, carry):
        k_own, v_own = sides(pair, p, 0.125)
        k_prev, v_prev = sides(prev, p, 0.125)
        dks, dvs = [], []
        for c in range(2):
            k_all = jnp.concatenate([k_own[c][0], k_prev[c][0], k_own[c][1], k_prev[c][1]], 0)
            v_all = jnp.concatenate([v_own[c][0], v_prev[c][0], v_own[c][1], v_prev[c][1]], 0)
            k_turned = k_all.T.astype(BF16)
            v_turned = v_all.T.astype(BF16)
            dk = [jnp.zeros((WINDOW, 128), F32)] * 2
            dv = [jnp.zeros((WINDOW, 128), F32)] * 2
            for half in range(2):
                at = p * 1024 + 512 * c + 256 * half
                q_rows, g_rows = stacked(query, at), stacked(grad, at)
                prob_all, slope_all = [], []
                for e in range(2):
                    unit = 4 * c + 2 * half + e
                    prob16, slope16 = probs[p, unit], slopes[p, unit]
                    prob_own, slope_own = prob16 * causal16, slope16 * causal16
                    dk[e] = dk[e] + dot(slope_own, q_rows, ((1,), (0,)))
                    dv[e] = dv[e] + dot(prob_own, g_rows, ((1,), (0,)))
                    prob_all += [prob_own, prob16 - prob_own]
                    slope_all += [slope_own, slope16 - slope_own]
                blended = dot(v_turned, jnp.concatenate(prob_all, 0), ((1,), (0,)))
                blended = jnp.where(alive, blended, 0.0)
                turned = dot(k_turned, jnp.concatenate(slope_all, 0), ((1,), (0,)))
                for q in range(2):
                    piece = slice(128 * q, 128 * q + 128)
                    attn_out[:, lanes_at(at + 128 * q)] = blended[:, piece].T.astype(BF16)
                    query_grad[:, lanes_at(at + 128 * q)] = turned[:, piece].T.astype(BF16)
            dks.append(dk)
            dvs.append(dv)
        own_k[:, lanes_at(p * 128)] = join_sides(dks, lo) * 0.125
        own_v[:, lanes_at(p * 128)] = join_sides(dvs, lo)
        return carry

    lax.fori_loop(0, PAIRS // 2, after, 0)
    total = give[rows_of(head), :].astype(F32)
    for t, copy in d_copies:
        copy.wait_recv()
        total = total + d_buf[t].astype(F32)
    slices = total[:, : 2 * KV]
    e_copies = []
    for s, who in earlier:
        e_send[s - 1] = jnp.where(tok - owner == s, slices, 0.0).astype(BF16)
        e_copies.append(ship(e_send.at[s - 1], e_recv.at[s - 1], e_sems, s - 1, who))
    sink_sum = total[:8, 2 * KV :] + total[8:, 2 * KV :]
    z_send[...] = sink_sum
    z_copies = [(t, ship(z_send, z_recv.at[t], z_sems, t, who)) for t, who in z_peers]
    lax.fori_loop(PAIRS // 2, PAIRS, after, 0)
    for copy in e_copies:
        copy.wait_recv()
    places = [tail_of(wrap(tok + s, RING), start, parent)[1] for s in range(1, LAG + 1)]
    arrived = [e_recv[s].astype(F32) for s in range(LAG)]

    def landed(place_):
        landing = jnp.zeros((ROWS, 2 * KV), F32)
        for s in range(LAG):
            landing = landing + jnp.where(places[s] == place_, arrived[s], 0.0)
        return landing.astype(BF16)

    f_copies = []
    for t, who in peers:
        f_send[t] = landed(who[1])
        f_copies.append(ship(f_send.at[t], f_recv.at[rows_of(head)], f_sems, t, who))
    f_recv[rows_of(head), :] = landed(head)
    for t, copy in z_copies:
        copy.wait_recv()
        sink_sum = sink_sum + z_recv[t]
    x_send[...] = sink_sum
    x_copies = [(t, ship(x_send, x_recv.at[t], x_sems, t, who)) for t, who in x_peers]
    back_copy.wait_recv()
    own_k[...] = own_k[...] + near_back[:, :KV].astype(F32)
    own_v[...] = own_v[...] + near_back[:, KV:].astype(F32)
    for copy in f_copies:
        copy.wait_recv()
    key_grad[...] = (own_k[...] + f_recv[:, :KV].astype(F32)).astype(BF16)
    value_grad[...] = (own_v[...] + f_recv[:, KV:].astype(F32)).astype(BF16)
    for t, copy in x_copies:
        copy.wait_recv()
        sink_sum = sink_sum + x_recv[t]
    sums = jnp.sum(sink_sum, axis=1, keepdims=True)
    line = jnp.sum(jnp.where(row == lane, sums, 0.0), axis=0)
    sink_grad[...] = -line[:8]
    for copy in sent:
        copy.wait_send()


def deliver(*refs):
    copies = [pltpu.make_async_copy(refs[n], refs[5 + n], refs[10].at[n]) for n in range(5)]
    for copy in copies:
        copy.start()
    for copy in copies:
        copy.wait()


RESULTS = (
    ((WINDOW, 4096), BF16),
    ((WINDOW, 4096), BF16),
    ((WINDOW, KV), BF16),
    ((WINDOW, KV), BF16),
    ((8,), F32),
)
SMEM = pl.BlockSpec(memory_space=pltpu.SMEM)
VMEM = pl.BlockSpec(memory_space=pltpu.VMEM)
HBM = pl.BlockSpec(memory_space=pltpu.HBM)
DMA = pltpu.SemaphoreType.DMA


def local(queries, key_states, value_states, out_grad, sink_logits, branch_start, branch_len, parent_list):
    block = pltpu.VMEM((WINDOW, 2 * KV), BF16)
    more = 2 * KV + 128
    three = pltpu.VMEM((LAG, ROWS, 2 * KV), BF16)
    rows = pltpu.VMEM((WINDOW, 4096), BF16)
    units = (PAIRS, 8, WINDOW, 256)
    results = pl.pallas_call(
        kernel,
        name="banded",
        out_shape=tuple(pltpu.VMEM(shape, kind) for shape, kind in RESULTS),
        in_specs=[SMEM] * 4 + [HBM] * 4,
        out_specs=(VMEM,) * 5,
        scratch_shapes=[
            rows, rows,
            pltpu.VMEM((WINDOW, more), BF16),
            pltpu.VMEM((GROUP, ROWS, more), BF16),
            block,
            three, three,
            pltpu.VMEM((ROWS, 2 * KV), BF16),
            block, block,
            pltpu.VMEM((GROUP, 8, 128), F32),
            pltpu.VMEM(units, F32), pltpu.VMEM(units, F32),
            pltpu.VMEM(units, BF16), pltpu.VMEM(units, BF16),
            pltpu.VMEM((WINDOW, KV), F32), pltpu.VMEM((WINDOW, KV), F32),
            pltpu.VMEM((WINDOW, more), BF16),
            pltpu.VMEM((GROUP, ROWS, more), BF16),
            block, block,
            three, three,
            pltpu.VMEM((GROUP, ROWS, 2 * KV), BF16),
            block,
            pltpu.VMEM((8, 128), F32), pltpu.VMEM((Z, 8, 128), F32),
            pltpu.VMEM((8, 128), F32), pltpu.VMEM((X, 8, 128), F32),
            pltpu.VMEM((GROUP, 8, 128), F32),
            DMA((4,)),
            DMA((2, GROUP)), DMA((2, 2)), DMA((2, LAG)), DMA((2, GROUP)),
            DMA((2, GROUP)), DMA((2, LAG)), DMA((2, GROUP)), DMA((2, Z)), DMA((2, X)),
        ],
        compiler_params=pltpu.CompilerParams(
            collective_id=0, has_side_effects=True, vmem_limit_bytes=58 * 1024 * 1024
        ),
    )(
        branch_start,
        branch_len,
        parent_list.T,
        sink_logits,
        *(pltpu.with_memory_space_constraint(x, pltpu.HBM) for x in (queries, out_grad, key_states, value_states)),
    )
    return pl.pallas_call(
        deliver,
        name="deliver",
        out_shape=tuple(jax.ShapeDtypeStruct(shape, kind) for shape, kind in RESULTS),
        in_specs=[VMEM] * 5,
        out_specs=(HBM,) * 5,
        scratch_shapes=[DMA((5,))],
    )(*(pltpu.with_memory_space_constraint(result, pltpu.VMEM) for result in results))


def solution(mesh):
    rows = P(("tok", "head"), None)
    return jax.shard_map(
        local,
        mesh=mesh,
        in_specs=(rows, rows, rows, rows, P("head"), P(), P(), P()),
        out_specs=(rows, rows, rows, rows, P("head")),
        check_vma=False,
    )
```

```python
import jax
import jax.numpy as jnp
from jax import lax
from jax.experimental import pallas as pl
from jax.experimental.pallas import tpu as pltpu
from jax.sharding import PartitionSpec as P

HEAD_DIM = 64
WINDOW = 128
LAG = 3
PAIRS = 4
BR_DEV = 2
GROUP = 8
RING = 32
ROWS = WINDOW // GROUP
KV = 512
Z = 8
X = 4
F32 = jnp.float32
BF16 = jnp.bfloat16
MESH = pl.DeviceIdType.MESH


def place():
    return lax.axis_index("tok"), lax.axis_index("head")


def block_state(tok, head, start, length, parent):
    pos = (tok * GROUP + head) * WINDOW
    alive, opening = False, False
    for b in range(BR_DEV):
        first = start[tok * BR_DEV + b]
        covers = (first <= pos) & (pos < first + length[tok * BR_DEV + b])
        alive = alive | covers
        opening = opening | (covers & (first == pos))
    return alive, opening, parent[0, tok * BR_DEV] >= 0


def tail_of(tok, start, parent):
    row = tok * BR_DEV
    token = start[jnp.maximum(parent[0, row], 0)] + parent[1, row]
    return lax.shift_right_logical(token, 10), lax.shift_right_logical(token, 7) & (GROUP - 1)


def send(src, dst, sems, slot, tok, head):
    copy = pltpu.make_async_remote_copy(
        src_ref=src,
        dst_ref=dst,
        send_sem=sems.at[0, slot],
        recv_sem=sems.at[1, slot],
        device_id=(tok, head),
        device_id_type=MESH,
    )
    copy.start()
    return copy


def wrap(value, count):
    return lax.rem(value + count, count)


def dot(left, right, dims):
    return lax.dot_general(left, right, (dims, ((), ())), preferred_element_type=F32)


def both_sides(block, lo):
    turned = pltpu.roll(block, HEAD_DIM, 1)
    zero = jnp.zeros_like(block)
    return (
        (jnp.where(lo, block, zero), jnp.where(lo, zero, turned)),
        (jnp.where(lo, turned, zero), jnp.where(lo, zero, block)),
    )


def join_sides(parts, lo):
    (a0, a1), (b0, b1) = parts
    return jnp.where(lo, a0, b1) + pltpu.roll(jnp.where(lo, b0, a1), HEAD_DIM, 1)


FAR_FIRST = (4, 5, 3, 6, 2, 7, 1)


def split_rows(rows):
    high = rows.astype(BF16).astype(F32)
    return jnp.concatenate([high, rows - high], 1).astype(BF16)


def kernel(
    start_in, length_in, parent_in, sink_in, queries, out_grad, keys, values,
    attn_out, query_grad, key_grad, value_grad, sink_grad,
    start, length, parent, sink, query, grad, pair, ak_buf, av_buf, near, b_send, bk_recv, bv_recv, mine, tail, prev, table,
    q_turned, g_turned, s_own, p_own, probs, slopes, own_k, own_v,
    give, dv_buf, dk_buf, near_send, near_back, e_send, e_recv, f_send, f_recv, z_send, z_recv, x_send, x_recv, part, lines,
    load_sems, a_sems, n_sems, b_sems, c_sems, d_sems, e_sems, f_sems, z_sems, x_sems,
):
    tok, head = place()
    x, z = tok // Z, lax.rem(tok, Z)
    peers = [(t, (tok, wrap(head + t, GROUP))) for t in FAR_FIRST]
    later = [(s, (wrap(tok + s, RING), head)) for s in (3, 2, 1)]
    earlier = [(s, (wrap(tok - s, RING), head)) for s in (3, 2, 1)]
    z_peers = [(t, (x * Z + wrap(z + t, Z), head)) for t in FAR_FIRST]
    x_peers = [(t, (wrap(x + t, X) * Z + z, head)) for t in (2, 3, 1)]
    right, left = (tok, wrap(head + 1, GROUP)), (tok, wrap(head - 1, GROUP))

    loads = [
        pltpu.make_async_copy(src, dst, load_sems.at[n])
        for n, (src, dst) in enumerate((
            (keys, pair.at[:, pl.ds(0, KV)]), (values, pair.at[:, pl.ds(KV, KV)]), (sink_in, sink), (start_in, start),
            (length_in, length), (parent_in, parent), (queries, query), (out_grad, grad),
        ))
    ]
    for load in loads:
        load.start()
    barrier = pltpu.get_barrier_semaphore()
    partners = [who for _, who in z_peers + later + earlier + peers + x_peers]
    for who in partners:
        pl.semaphore_signal(barrier, inc=1, device_id=who, device_id_type=MESH)

    for load in loads[2:6]:
        load.wait()
    alive, opening, rooted = block_state(tok, head, start, length, parent)
    ok = alive & (jnp.logical_not(opening) | rooted)
    outward = opening & rooted
    inward = alive & jnp.logical_not(opening)
    row = lax.broadcasted_iota(jnp.int32, (8, 128), 0)
    lane = lax.broadcasted_iota(jnp.int32, (8, 128), 1)
    sink_tile = jnp.zeros((8, 128), F32)
    for g in range(8):
        sink_tile = jnp.where(row == g, sink[g], sink_tile)
    table[head] = sink_tile
    pair[:, 2 * KV :] = split_rows(jnp.broadcast_to(sink_tile[None], (GROUP, 8, 128))).reshape(WINDOW, 128)
    loads[0].wait()
    loads[1].wait()
    pl.semaphore_wait(barrier, len(partners))

    def rows_of(place_):
        return pl.ds(pl.multiple_of(place_ * ROWS, ROWS), ROWS)

    sent = []

    def ship(src, dst, sems, slot, who):
        copy = send(src, dst, sems, slot, *who)
        sent.append(copy)
        return copy

    keys_at, values_at = pl.ds(0, KV), pl.ds(KV, KV)
    ak_copies = [ship(pair.at[rows_of(who[1]), keys_at], ak_buf.at[t], a_sems, t, who) for t, who in peers]
    av_copies = [
        ship(pair.at[rows_of(who[1]), pl.ds(KV, KV + 128)], av_buf.at[t], a_sems, GROUP + t, who) for t, who in peers
    ]
    ak_buf[0] = pair[rows_of(head), :KV]
    av_buf[0] = pair[rows_of(head), KV:]

    lo = lax.broadcasted_iota(jnp.int32, (WINDOW, 128), 1) < HEAD_DIM
    place_j = lax.broadcasted_iota(jnp.int32, (WINDOW, 256), 0)
    place_i = lax.broadcasted_iota(jnp.int32, (WINDOW, 256), 1) & (WINDOW - 1)
    causal = place_j <= place_i
    causal16 = causal.astype(F32).astype(BF16)
    bias = jnp.where(ok, 0.0, -jnp.inf)

    def lanes_at(at, size=128):
        return pl.ds(pl.multiple_of(at, size), size)

    def sides(ref, p, factor):
        k = both_sides(ref[:, lanes_at(p * 128)].astype(F32) * factor, lo)
        v = both_sides(ref[:, lanes_at(KV + p * 128)].astype(F32), lo)
        return k, v

    def stacked(ref, at):
        return jnp.concatenate([ref[:, lanes_at(at)], ref[:, lanes_at(at + 128)]], 0)

    def both_rows(sides_):
        return jnp.concatenate([side.astype(BF16) for side in sides_], 0)

    def before(p, carry):
        wide = lanes_at(p * 1024, 1024)
        grad[:, wide] = jnp.where(alive, grad[:, wide], jnp.zeros((), BF16))
        k, v = sides(pair, p, 0.125)
        for c in range(2):
            k_rows, v_rows = both_rows(k[c]), both_rows(v[c])
            for half in range(2):
                at = p * 1024 + 512 * c + 256 * half
                for ref, turned_ref, rows, own in (
                    (query, q_turned, k_rows, s_own), (grad, g_turned, v_rows, p_own)
                ):
                    turned = jnp.concatenate([ref[:, lanes_at(at + 128 * q)].T for q in range(2)], 1)
                    turned_ref[p, 2 * c + half] = turned
                    own[p, 2 * c + half] = dot(rows, turned, ((1,), (0,)))
        return carry

    loads[6].wait()
    loads[7].wait()
    lax.fori_loop(0, PAIRS // 2, before, 0)

    tails = [(s, who, (head - tail_of(who[0], start, parent)[1]) & (GROUP - 1)) for s, who in later]

    def pass_on(a_buf, b_recv, chunk):
        copies = []
        for s, who, slot in tails:
            b_send[chunk, s - 1] = a_buf[slot][:, :KV]
            copies.append(ship(b_send.at[chunk, s - 1], b_recv.at[s - 1], b_sems, LAG * chunk + s - 1, who))
        return copies

    for copy in ak_copies:
        copy.wait_recv()
    bk_copies = pass_on(ak_buf, bk_recv, 0)
    for copy in av_copies:
        copy.wait_recv()
    bv_copies = pass_on(av_buf, bv_recv, 1)
    near_copies = [
        ship(pair.at[:, at], near.at[:, at], n_sems, n, right) for n, at in enumerate((keys_at, values_at))
    ]
    for t in range(1, GROUP):
        extra = av_buf[t, :, KV:].astype(F32)
        table[wrap(head - t, GROUP)] = extra[:8] + extra[8:]
    for h in range(GROUP):
        for line in range(4):
            first = 4 * (line // 2) + line % 2
            both = [table[h, first + 2 * q : first + 2 * q + 1, :] for q in range(2)]
            at = 4 * (h % 2) + line
            lines[h // 2, at : at + 1, :] = jnp.concatenate(both, 1)
    lax.fori_loop(PAIRS // 2, PAIRS, before, 0)
    owner, _ = tail_of(tok, start, parent)
    behind = jnp.clip(tok - owner - 1, 0, LAG - 1)

    def spread(copies, b_recv, chunk, at):
        for copy in copies:
            copy.wait_recv()
        mine[chunk] = b_recv[behind]
        tail[rows_of(head), at] = mine[chunk]
        return [
            ship(mine.at[chunk], tail.at[rows_of(head), at], c_sems, GROUP * chunk + t, who) for t, who in peers
        ]

    ck_copies = spread(bk_copies, bk_recv, 0, keys_at)
    cv_copies = spread(bv_copies, bv_recv, 1, values_at)

    def choose(copies, near_copy, at):
        near_copy.wait_recv()
        for copy in copies:
            copy.wait_recv()
        prev[:, at] = jnp.where(ok, jnp.where(opening, tail[:, at], near[:, at]), jnp.zeros((), BF16))

    choose(ck_copies, near_copies[0], keys_at)

    zero16 = jnp.zeros((), BF16)

    def hand(p, block, give_at, near_at):
        block = block.astype(BF16)
        give[:, lanes_at(give_at + p * 128)] = jnp.where(outward, block, zero16)
        near_send[:, lanes_at(near_at + p * 128)] = jnp.where(inward, block, zero16)

    def weigh(p, carry):
        k = both_sides(prev[:, lanes_at(p * 128)].astype(F32) * 0.125, lo)
        dvs = []
        for c in range(2):
            k_rows = both_rows(k[c])
            dv = jnp.zeros((256, 128), F32)
            for half in range(2):
                unit = 2 * c + half
                g_rows = stacked(grad, p * 1024 + 512 * c + 256 * half)
                scores_both = dot(k_rows, q_turned[p, unit], ((1,), (0,)))
                behind16 = []
                for e in range(2):
                    at, line = slice(128 * e, 128 * e + 128), 2 * unit + e
                    scores = jnp.where(causal, s_own[p, unit, at], scores_both[at] + bias)
                    sinks = lines[p, line : line + 1, :]
                    peak = jnp.maximum(jnp.max(scores, axis=0, keepdims=True), sinks)
                    exps = jnp.exp(scores - peak)
                    sink_exp = jnp.exp(sinks - peak)
                    inverse = 1.0 / (jnp.sum(exps, axis=0, keepdims=True) + sink_exp)
                    prob = exps * inverse
                    s_own[p, unit, at] = prob
                    part[p, line : line + 1, :] = sink_exp * inverse
                    prob16 = prob.astype(BF16)
                    probs[p, unit, at] = prob16
                    behind16.append(prob16 - prob16 * causal16)
                dv = dv + dot(jnp.concatenate(behind16, 0), g_rows, ((1,), (0,)))
            dvs.append((dv[:WINDOW], dv[WINDOW:]))
        hand(p, join_sides(dvs, lo), 0, KV)
        return carry

    lax.fori_loop(0, PAIRS, weigh, 0)
    dv_copies = [ship(give.at[rows_of(who[1]), pl.ds(0, KV)], dv_buf.at[t], d_sems, t, who) for t, who in peers]
    back_copies = [ship(near_send.at[:, values_at], near_back.at[:, values_at], n_sems, 2, left)]
    choose(cv_copies, near_copies[1], values_at)

    def incline(p, carry):
        v = both_sides(prev[:, lanes_at(KV + p * 128)].astype(F32), lo)
        dks = []
        for c in range(2):
            v_rows = both_rows(v[c])
            dk = jnp.zeros((256, 128), F32)
            for half in range(2):
                unit = 2 * c + half
                q_rows = stacked(query, p * 1024 + 512 * c + 256 * half)
                inner_both = dot(v_rows, g_turned[p, unit], ((1,), (0,)))
                behind16 = []
                for e in range(2):
                    at, line = slice(128 * e, 128 * e + 128), 2 * unit + e
                    inner = jnp.where(causal, p_own[p, unit, at], inner_both[at])
                    prob = s_own[p, unit, at]
                    weighed = prob * inner
                    delta = jnp.sum(weighed, axis=0, keepdims=True)
                    slope16 = (weighed - prob * delta).astype(BF16)
                    part[p, line : line + 1, :] = part[p, line : line + 1, :] * delta
                    slopes[p, unit, at] = slope16
                    behind16.append(slope16 - slope16 * causal16)
                dk = dk + dot(jnp.concatenate(behind16, 0), q_rows, ((1,), (0,)))
            dks.append((dk[:WINDOW], dk[WINDOW:]))
        hand(p, join_sides(dks, lo) * 0.125, KV, 0)
        return carry

    lax.fori_loop(0, PAIRS, incline, 0)
    terms = part[...].reshape(GROUP, 4, 256)
    terms = jnp.concatenate([terms[:, :, :128], terms[:, :, 128:]], 1)
    give[:, 2 * KV :] = split_rows(terms).reshape(WINDOW, 128)
    dk_copies = [
        ship(give.at[rows_of(who[1]), pl.ds(KV, KV + 128)], dk_buf.at[t], d_sems, GROUP + t, who) for t, who in peers
    ]

    def after(p, carry):
        k_own, v_own = sides(pair, p, 0.125)
        k_prev, v_prev = sides(prev, p, 0.125)
        dks, dvs = [], []
        for c in range(2):
            k_all = jnp.concatenate([k_own[c][0], k_prev[c][0], k_own[c][1], k_prev[c][1]], 0)
            v_all = jnp.concatenate([v_own[c][0], v_prev[c][0], v_own[c][1], v_prev[c][1]], 0)
            k_turned = k_all.T.astype(BF16)
            v_turned = v_all.T.astype(BF16)
            dk, dv = jnp.zeros((256, 128), F32), jnp.zeros((256, 128), F32)
            for half in range(2):
                at, unit = p * 1024 + 512 * c + 256 * half, 2 * c + half
                q_rows, g_rows = stacked(query, at), stacked(grad, at)
                prob_all, slope_all, prob_own, slope_own = [], [], [], []
                for e in range(2):
                    prob16 = probs[p, unit, 128 * e : 128 * e + 128]
                    slope16 = slopes[p, unit, 128 * e : 128 * e + 128]
                    prob_own.append(prob16 * causal16)
                    slope_own.append(slope16 * causal16)
                    prob_all += [prob_own[e], prob16 - prob_own[e]]
                    slope_all += [slope_own[e], slope16 - slope_own[e]]
                dk = dk + dot(jnp.concatenate(slope_own, 0), q_rows, ((1,), (0,)))
                dv = dv + dot(jnp.concatenate(prob_own, 0), g_rows, ((1,), (0,)))
                blended = dot(v_turned, jnp.concatenate(prob_all, 0), ((1,), (0,)))
                blended = jnp.where(alive, blended, 0.0)
                turned = dot(k_turned, jnp.concatenate(slope_all, 0), ((1,), (0,)))
                for q in range(2):
                    piece = slice(128 * q, 128 * q + 128)
                    attn_out[:, lanes_at(at + 128 * q)] = blended[:, piece].T.astype(BF16)
                    query_grad[:, lanes_at(at + 128 * q)] = turned[:, piece].T.astype(BF16)
            dks.append((dk[:WINDOW], dk[WINDOW:]))
            dvs.append((dv[:WINDOW], dv[WINDOW:]))
        own_k[:, lanes_at(p * 128)] = join_sides(dks, lo) * 0.125
        own_v[:, lanes_at(p * 128)] = join_sides(dvs, lo)
        return carry

    def gather(copies, own, d_buf):
        total = own.astype(F32)
        for (t, _), copy in zip(peers, copies):
            copy.wait_recv()
            total = total + d_buf[t].astype(F32)
        return total

    def send_back(slices, chunk):
        copies = []
        for s, who in earlier:
            e_send[chunk, s - 1] = jnp.where(tok - owner == s, slices, 0.0).astype(BF16)
            copies.append(ship(e_send.at[chunk, s - 1], e_recv.at[chunk, s - 1], e_sems, LAG * chunk + s - 1, who))
        return copies

    ev_copies = send_back(gather(dv_copies, give[rows_of(head), :KV], dv_buf), 1)
    lax.fori_loop(0, 1, after, 0)
    total = gather(dk_copies, give[rows_of(head), KV:], dk_buf)
    ek_copies = send_back(total[:, :KV], 0)
    sink_sum = total[:8, KV:] + total[8:, KV:]
    z_send[...] = sink_sum
    z_copies = [(t, ship(z_send, z_recv.at[t], z_sems, t, who)) for t, who in z_peers]
    back_copies.append(ship(near_send.at[:, keys_at], near_back.at[:, keys_at], n_sems, 3, left))
    lax.fori_loop(1, 3, after, 0)
    places = [tail_of(wrap(tok + s, RING), start, parent)[1] for s in range(1, LAG + 1)]

    def land(copies, chunk, at):
        for copy in copies:
            copy.wait_recv()
        arrived = [e_recv[chunk, s].astype(F32) for s in range(LAG)]

        def landed(place_):
            landing = jnp.zeros((ROWS, KV), F32)
            for s in range(LAG):
                landing = landing + jnp.where(places[s] == place_, arrived[s], 0.0)
            return landing.astype(BF16)

        copies = []
        for t, who in peers:
            f_send[chunk, t] = landed(who[1])
            copies.append(ship(f_send.at[chunk, t], f_recv.at[rows_of(head), at], f_sems, GROUP * chunk + t, who))
        f_recv[rows_of(head), at] = landed(head)
        return copies

    f_copies = land(ev_copies, 1, values_at)
    lax.fori_loop(3, PAIRS, after, 0)
    f_copies += land(ek_copies, 0, keys_at)
    for t, copy in z_copies:
        copy.wait_recv()
        sink_sum = sink_sum + z_recv[t]
    x_send[...] = sink_sum
    x_copies = [(t, ship(x_send, x_recv.at[t], x_sems, t, who)) for t, who in x_peers]
    for copy in back_copies:
        copy.wait_recv()
    own_k[...] = own_k[...] + near_back[:, :KV].astype(F32)
    own_v[...] = own_v[...] + near_back[:, KV:].astype(F32)
    for copy in f_copies:
        copy.wait_recv()
    key_grad[...] = (own_k[...] + f_recv[:, :KV].astype(F32)).astype(BF16)
    value_grad[...] = (own_v[...] + f_recv[:, KV:].astype(F32)).astype(BF16)
    for t, copy in x_copies:
        copy.wait_recv()
        sink_sum = sink_sum + x_recv[t]
    sums = jnp.sum(sink_sum, axis=1, keepdims=True)
    place_ = 4 * ((row >> 1) & 1) + 2 * (row >> 2) + (row & 1)
    line = jnp.sum(jnp.where(place_ == lane, sums, 0.0), axis=0)
    sink_grad[...] = -line[:8]
    for copy in sent:
        copy.wait_send()


def deliver(*refs):
    copies = [pltpu.make_async_copy(refs[n], refs[5 + n], refs[10].at[n]) for n in range(5)]
    for copy in copies:
        copy.start()
    for copy in copies:
        copy.wait()


RESULTS = (
    ((WINDOW, 4096), BF16),
    ((WINDOW, 4096), BF16),
    ((WINDOW, KV), BF16),
    ((WINDOW, KV), BF16),
    ((8,), F32),
)
VMEM = pl.BlockSpec(memory_space=pltpu.VMEM)
HBM = pl.BlockSpec(memory_space=pltpu.HBM)
DMA = pltpu.SemaphoreType.DMA


def local(queries, key_states, value_states, out_grad, sink_logits, branch_start, branch_len, parent_list):
    block = pltpu.VMEM((WINDOW, 2 * KV), BF16)
    slices = pltpu.VMEM((GROUP, ROWS, KV), BF16)
    slices_more = pltpu.VMEM((GROUP, ROWS, KV + 128), BF16)
    three = pltpu.VMEM((2, LAG, ROWS, KV), BF16)
    rows = pltpu.VMEM((WINDOW, 4096), BF16)
    units = (PAIRS, 4, 2 * WINDOW, 256)
    turned = pltpu.VMEM((PAIRS, 4, 128, 256), BF16)
    results = pl.pallas_call(
        kernel,
        name="banded",
        out_shape=tuple(pltpu.VMEM(shape, kind) for shape, kind in RESULTS),
        in_specs=[HBM] * 8,
        out_specs=(VMEM,) * 5,
        scratch_shapes=[
            pltpu.SMEM((64,), jnp.int32), pltpu.SMEM((64,), jnp.int32),
            pltpu.SMEM((2, 64), jnp.int32), pltpu.SMEM((8,), F32),
            rows, rows,
            pltpu.VMEM((WINDOW, 2 * KV + 128), BF16),
            slices, slices_more,
            block,
            three,
            pltpu.VMEM((LAG, ROWS, KV), BF16), pltpu.VMEM((LAG, ROWS, KV), BF16),
            pltpu.VMEM((2, ROWS, KV), BF16),
            block, block,
            pltpu.VMEM((GROUP, 8, 128), F32),
            turned, turned,
            pltpu.VMEM(units, F32), pltpu.VMEM(units, F32),
            pltpu.VMEM(units, BF16), pltpu.VMEM(units, BF16),
            pltpu.VMEM((WINDOW, KV), F32), pltpu.VMEM((WINDOW, KV), F32),
            pltpu.VMEM((WINDOW, 2 * KV + 128), BF16),
            slices, slices_more,
            block, block,
            three, three,
            pltpu.VMEM((2, GROUP, ROWS, KV), BF16),
            block,
            pltpu.VMEM((8, 128), F32), pltpu.VMEM((Z, 8, 128), F32),
            pltpu.VMEM((8, 128), F32), pltpu.VMEM((X, 8, 128), F32),
            pltpu.VMEM((PAIRS, 8, 256), F32), pltpu.VMEM((PAIRS, 8, 256), F32),
            DMA((8,)),
            DMA((2, 2 * GROUP)), DMA((2, 4)), DMA((2, 2 * LAG)), DMA((2, 2 * GROUP)),
            DMA((2, 2 * GROUP)), DMA((2, 2 * LAG)), DMA((2, 2 * GROUP)), DMA((2, Z)), DMA((2, X)),
        ],
        compiler_params=pltpu.CompilerParams(
            collective_id=0, has_side_effects=True, vmem_limit_bytes=58 * 1024 * 1024
        ),
    )(
        *(
            pltpu.with_memory_space_constraint(x, pltpu.HBM)
            for x in (
                branch_start, branch_len, parent_list.T, sink_logits, queries, out_grad, key_states, value_states
            )
        ),
    )
    return pl.pallas_call(
        deliver,
        name="deliver",
        out_shape=tuple(jax.ShapeDtypeStruct(shape, kind) for shape, kind in RESULTS),
        in_specs=[VMEM] * 5,
        out_specs=(HBM,) * 5,
        scratch_shapes=[DMA((5,))],
    )(*(pltpu.with_memory_space_constraint(result, pltpu.VMEM) for result in results))


def solution(mesh):
    rows = P(("tok", "head"), None)
    return jax.shard_map(
        local,
        mesh=mesh,
        in_specs=(rows, rows, rows, rows, P("head"), P(), P(), P()),
        out_specs=(rows, rows, rows, rows, P("head")),
        check_vma=False,
    )
```

```python
import jax
import jax.numpy as jnp
from jax import lax
from jax.experimental import pallas as pl
from jax.experimental.pallas import tpu as pltpu
from jax.sharding import PartitionSpec as P

HEAD_DIM = 64
WINDOW = 128
LAG = 3
CHUNKS = 4
PART = 256
PAIRS = 4
BR_DEV = 2
GROUP = 8
RING = 32
ROWS = WINDOW // GROUP
KV = 512
Z = 8
X = 4
F32 = jnp.float32
BF16 = jnp.bfloat16
MESH = pl.DeviceIdType.MESH


def place():
    return lax.axis_index("tok"), lax.axis_index("head")


def block_state(tok, head, start, length, parent):
    pos = (tok * GROUP + head) * WINDOW
    alive, opening = False, False
    for b in range(BR_DEV):
        first = start[tok * BR_DEV + b]
        covers = (first <= pos) & (pos < first + length[tok * BR_DEV + b])
        alive = alive | covers
        opening = opening | (covers & (first == pos))
    return alive, opening, parent[0, tok * BR_DEV] >= 0


def tail_of(tok, start, parent):
    row = tok * BR_DEV
    token = start[jnp.maximum(parent[0, row], 0)] + parent[1, row]
    return lax.shift_right_logical(token, 10), lax.shift_right_logical(token, 7) & (GROUP - 1)


def send(src, dst, sems, slot, tok, head):
    copy = pltpu.make_async_remote_copy(
        src_ref=src,
        dst_ref=dst,
        send_sem=sems.at[0, slot],
        recv_sem=sems.at[1, slot],
        device_id=(tok, head),
        device_id_type=MESH,
    )
    copy.start()
    return copy


def wrap(value, count):
    return lax.rem(value + count, count)


def dot(left, right, dims):
    return lax.dot_general(left, right, (dims, ((), ())), preferred_element_type=F32)


def both_sides(block, lo):
    turned = pltpu.roll(block, HEAD_DIM, 1)
    zero = jnp.zeros_like(block)
    return (
        (jnp.where(lo, block, zero), jnp.where(lo, zero, turned)),
        (jnp.where(lo, turned, zero), jnp.where(lo, zero, block)),
    )


def join_sides(parts, lo):
    (a0, a1), (b0, b1) = parts
    return jnp.where(lo, a0, b1) + pltpu.roll(jnp.where(lo, b0, a1), HEAD_DIM, 1)


FAR_FIRST = (4, 5, 3, 6, 2, 7, 1)


def split_rows(rows):
    high = rows.astype(BF16).astype(F32)
    return jnp.concatenate([high, rows - high], 1).astype(BF16)


def kernel(
    start_in, length_in, parent_in, sink_in, queries, out_grad, keys, values,
    attn_out, query_grad, key_grad, value_grad, sink_grad,
    start, length, parent, sink, query, grad, pair, a0, a1, a2, a3, near, b_send, b0, b1, b2, b3, mine, tail, prev, table,
    q_turned, g_turned, s_own, p_own, probs, slopes, own_k, own_v,
    give, d_buf, near_send, near_back, e_send, e_recv, f_send, f_recv, z_send, z_recv, x_send, x_recv, part, lines,
    load_sems, a_sems, n_sems, b_sems, c_sems, d_sems, e_sems, f_sems, z_sems, x_sems,
):
    tok, head = place()
    x, z = tok // Z, lax.rem(tok, Z)
    peers = [(t, (tok, wrap(head + t, GROUP))) for t in FAR_FIRST]
    later = [(s, (wrap(tok + s, RING), head)) for s in (3, 2, 1)]
    earlier = [(s, (wrap(tok - s, RING), head)) for s in (3, 2, 1)]
    z_peers = [(t, (x * Z + wrap(z + t, Z), head)) for t in FAR_FIRST]
    x_peers = [(t, (wrap(x + t, X) * Z + z, head)) for t in (2, 3, 1)]
    right, left = (tok, wrap(head + 1, GROUP)), (tok, wrap(head - 1, GROUP))

    loads = [
        pltpu.make_async_copy(src, dst, load_sems.at[n])
        for n, (src, dst) in enumerate((
            (keys, pair.at[:, pl.ds(0, KV)]), (values, pair.at[:, pl.ds(KV, KV)]), (sink_in, sink), (start_in, start),
            (length_in, length), (parent_in, parent), (queries, query), (out_grad, grad),
        ))
    ]
    for load in loads:
        load.start()
    barrier = pltpu.get_barrier_semaphore()
    partners = [who for _, who in z_peers + later + earlier + peers + x_peers]
    for who in partners:
        pl.semaphore_signal(barrier, inc=1, device_id=who, device_id_type=MESH)

    for load in loads[2:6]:
        load.wait()
    alive, opening, rooted = block_state(tok, head, start, length, parent)
    ok = alive & (jnp.logical_not(opening) | rooted)
    outward = opening & rooted
    inward = alive & jnp.logical_not(opening)
    row = lax.broadcasted_iota(jnp.int32, (8, 128), 0)
    lane = lax.broadcasted_iota(jnp.int32, (8, 128), 1)
    sink_tile = jnp.zeros((8, 128), F32)
    for g in range(8):
        sink_tile = jnp.where(row == g, sink[g], sink_tile)
    table[head] = sink_tile
    pair[:, 2 * KV :] = split_rows(jnp.broadcast_to(sink_tile[None], (GROUP, 8, 128))).reshape(WINDOW, 128)
    loads[0].wait()
    loads[1].wait()
    pl.semaphore_wait(barrier, len(partners))

    def rows_of(place_):
        return pl.ds(pl.multiple_of(place_ * ROWS, ROWS), ROWS)

    sent = []

    def ship(src, dst, sems, slot, who):
        copy = send(src, dst, sems, slot, *who)
        sent.append(copy)
        return copy

    keys_at, values_at = pl.ds(0, KV), pl.ds(KV, KV)
    a_bufs, b_recvs = (a0, a1, a2, a3), (b0, b1, b2, b3)

    def chunk_at(n):
        return pl.ds(PART * n, PART)

    def wide_at(n):
        return pl.ds(PART * n, PART + 128 if n == CHUNKS - 1 else PART)

    a_copies = [
        [ship(pair.at[rows_of(who[1]), wide_at(n)], a_bufs[n].at[t], a_sems, GROUP * n + t, who) for t, who in peers]
        for n in range(CHUNKS)
    ]
    for n in range(CHUNKS):
        a_bufs[n][0] = pair[rows_of(head), wide_at(n)]

    lo = lax.broadcasted_iota(jnp.int32, (WINDOW, 128), 1) < HEAD_DIM
    place_j = lax.broadcasted_iota(jnp.int32, (WINDOW, 256), 0)
    place_i = lax.broadcasted_iota(jnp.int32, (WINDOW, 256), 1) & (WINDOW - 1)
    causal = place_j <= place_i
    causal16 = causal.astype(F32).astype(BF16)
    bias = jnp.where(ok, 0.0, -jnp.inf)

    def lanes_at(at, size=128):
        return pl.ds(pl.multiple_of(at, size), size)

    def sides(ref, p, factor):
        k = both_sides(ref[:, lanes_at(p * 128)].astype(F32) * factor, lo)
        v = both_sides(ref[:, lanes_at(KV + p * 128)].astype(F32), lo)
        return k, v

    def stacked(ref, at):
        return jnp.concatenate([ref[:, lanes_at(at)], ref[:, lanes_at(at + 128)]], 0)

    def both_rows(sides_):
        return jnp.concatenate([side.astype(BF16) for side in sides_], 0)

    def before(p, carry):
        wide = lanes_at(p * 1024, 1024)
        grad[:, wide] = jnp.where(alive, grad[:, wide], jnp.zeros((), BF16))
        k, v = sides(pair, p, 0.125)
        for c in range(2):
            k_rows, v_rows = both_rows(k[c]), both_rows(v[c])
            for half in range(2):
                at = p * 1024 + 512 * c + 256 * half
                for ref, turned_ref, rows, own in (
                    (query, q_turned, k_rows, s_own), (grad, g_turned, v_rows, p_own)
                ):
                    turned = jnp.concatenate([ref[:, lanes_at(at + 128 * q)].T for q in range(2)], 1)
                    turned_ref[p, 2 * c + half] = turned
                    own[p, 2 * c + half] = dot(rows, turned, ((1,), (0,)))
        return carry

    loads[6].wait()
    loads[7].wait()
    lax.fori_loop(0, PAIRS // 2, before, 0)

    tails = [(s, who, (head - tail_of(who[0], start, parent)[1]) & (GROUP - 1)) for s, who in later]

    b_copies = []
    for n in range(CHUNKS):
        for copy in a_copies[n]:
            copy.wait_recv()
        b_copies.append([])
        for s, who, slot in tails:
            b_send[n, s - 1] = a_bufs[n][slot][:, :PART]
            b_copies[n].append(ship(b_send.at[n, s - 1], b_recvs[n].at[s - 1], b_sems, LAG * n + s - 1, who))
    near_copies = [
        ship(pair.at[:, at], near.at[:, at], n_sems, n, right) for n, at in enumerate((keys_at, values_at))
    ]
    for t in range(1, GROUP):
        extra = a3[t, :, PART:].astype(F32)
        table[wrap(head - t, GROUP)] = extra[:8] + extra[8:]
    for h in range(GROUP):
        for line in range(4):
            first = 4 * (line // 2) + line % 2
            both = [table[h, first + 2 * q : first + 2 * q + 1, :] for q in range(2)]
            at = 4 * (h % 2) + line
            lines[h // 2, at : at + 1, :] = jnp.concatenate(both, 1)
    lax.fori_loop(PAIRS // 2, PAIRS, before, 0)
    owner, _ = tail_of(tok, start, parent)
    behind = jnp.clip(tok - owner - 1, 0, LAG - 1)

    c_copies = []
    for n in range(CHUNKS):
        for copy in b_copies[n]:
            copy.wait_recv()
        mine[n] = b_recvs[n][behind]
        tail[rows_of(head), chunk_at(n)] = mine[n]
        c_copies.append([
            ship(mine.at[n], tail.at[rows_of(head), chunk_at(n)], c_sems, GROUP * n + t, who) for t, who in peers
        ])

    def choose(n):
        if n % 2 == 0:
            near_copies[n // 2].wait_recv()
        for copy in c_copies[n]:
            copy.wait_recv()
        at = chunk_at(n)
        prev[:, at] = jnp.where(ok, jnp.where(opening, tail[:, at], near[:, at]), jnp.zeros((), BF16))

    def gather_from(n):
        return [
            ship(give.at[rows_of(who[1]), wide_at(n)], d_buf.at[n, t, :, pl.ds(0, PART + 128 if n == CHUNKS - 1 else PART)],
                 d_sems, GROUP * n + t, who)
            for t, who in peers
        ]

    zero16 = jnp.zeros((), BF16)

    def hand(p, block, give_at, near_at):
        block = block.astype(BF16)
        give[:, lanes_at(give_at + p * 128)] = jnp.where(outward, block, zero16)
        near_send[:, lanes_at(near_at + p * 128)] = jnp.where(inward, block, zero16)

    def weigh(p, carry):
        k = both_sides(prev[:, lanes_at(p * 128)].astype(F32) * 0.125, lo)
        dvs = []
        for c in range(2):
            k_rows = both_rows(k[c])
            dv = jnp.zeros((256, 128), F32)
            for half in range(2):
                unit = 2 * c + half
                g_rows = stacked(grad, p * 1024 + 512 * c + 256 * half)
                scores_both = dot(k_rows, q_turned[p, unit], ((1,), (0,)))
                behind16 = []
                for e in range(2):
                    at, line = slice(128 * e, 128 * e + 128), 2 * unit + e
                    scores = jnp.where(causal, s_own[p, unit, at], scores_both[at] + bias)
                    sinks = lines[p, line : line + 1, :]
                    peak = jnp.maximum(jnp.max(scores, axis=0, keepdims=True), sinks)
                    exps = jnp.exp(scores - peak)
                    sink_exp = jnp.exp(sinks - peak)
                    inverse = 1.0 / (jnp.sum(exps, axis=0, keepdims=True) + sink_exp)
                    prob = exps * inverse
                    s_own[p, unit, at] = prob
                    part[p, line : line + 1, :] = sink_exp * inverse
                    prob16 = prob.astype(BF16)
                    probs[p, unit, at] = prob16
                    behind16.append(prob16 - prob16 * causal16)
                dv = dv + dot(jnp.concatenate(behind16, 0), g_rows, ((1,), (0,)))
            dvs.append((dv[:WINDOW], dv[WINDOW:]))
        hand(p, join_sides(dvs, lo), 0, KV)
        return carry

    d_copies = []
    for n in range(2):
        choose(n)
        lax.fori_loop(2 * n, 2 * n + 2, weigh, 0)
        d_copies.append(gather_from(n))
    back_copies = [ship(near_send.at[:, values_at], near_back.at[:, values_at], n_sems, 2, left)]

    def incline(p, carry):
        v = both_sides(prev[:, lanes_at(KV + p * 128)].astype(F32), lo)
        dks = []
        for c in range(2):
            v_rows = both_rows(v[c])
            dk = jnp.zeros((256, 128), F32)
            for half in range(2):
                unit = 2 * c + half
                q_rows = stacked(query, p * 1024 + 512 * c + 256 * half)
                inner_both = dot(v_rows, g_turned[p, unit], ((1,), (0,)))
                behind16 = []
                for e in range(2):
                    at, line = slice(128 * e, 128 * e + 128), 2 * unit + e
                    inner = jnp.where(causal, p_own[p, unit, at], inner_both[at])
                    prob = s_own[p, unit, at]
                    weighed = prob * inner
                    delta = jnp.sum(weighed, axis=0, keepdims=True)
                    slope16 = (weighed - prob * delta).astype(BF16)
                    part[p, line : line + 1, :] = part[p, line : line + 1, :] * delta
                    slopes[p, unit, at] = slope16
                    behind16.append(slope16 - slope16 * causal16)
                dk = dk + dot(jnp.concatenate(behind16, 0), q_rows, ((1,), (0,)))
            dks.append((dk[:WINDOW], dk[WINDOW:]))
        hand(p, join_sides(dks, lo) * 0.125, KV, 0)
        return carry

    choose(2)
    lax.fori_loop(0, 2, incline, 0)
    d_copies.append(gather_from(2))
    choose(3)
    lax.fori_loop(2, PAIRS, incline, 0)
    terms = part[...].reshape(GROUP, 4, 256)
    terms = jnp.concatenate([terms[:, :, :128], terms[:, :, 128:]], 1)
    give[:, 2 * KV :] = split_rows(terms).reshape(WINDOW, 128)
    d_copies.append(gather_from(3))

    def after(p, carry):
        k_own, v_own = sides(pair, p, 0.125)
        k_prev, v_prev = sides(prev, p, 0.125)
        dks, dvs = [], []
        for c in range(2):
            k_all = jnp.concatenate([k_own[c][0], k_prev[c][0], k_own[c][1], k_prev[c][1]], 0)
            v_all = jnp.concatenate([v_own[c][0], v_prev[c][0], v_own[c][1], v_prev[c][1]], 0)
            k_turned = k_all.T.astype(BF16)
            v_turned = v_all.T.astype(BF16)
            dk, dv = jnp.zeros((256, 128), F32), jnp.zeros((256, 128), F32)
            for half in range(2):
                at, unit = p * 1024 + 512 * c + 256 * half, 2 * c + half
                q_rows, g_rows = stacked(query, at), stacked(grad, at)
                prob_all, slope_all, prob_own, slope_own = [], [], [], []
                for e in range(2):
                    prob16 = probs[p, unit, 128 * e : 128 * e + 128]
                    slope16 = slopes[p, unit, 128 * e : 128 * e + 128]
                    prob_own.append(prob16 * causal16)
                    slope_own.append(slope16 * causal16)
                    prob_all += [prob_own[e], prob16 - prob_own[e]]
                    slope_all += [slope_own[e], slope16 - slope_own[e]]
                dk = dk + dot(jnp.concatenate(slope_own, 0), q_rows, ((1,), (0,)))
                dv = dv + dot(jnp.concatenate(prob_own, 0), g_rows, ((1,), (0,)))
                blended = dot(v_turned, jnp.concatenate(prob_all, 0), ((1,), (0,)))
                blended = jnp.where(alive, blended, 0.0)
                turned = dot(k_turned, jnp.concatenate(slope_all, 0), ((1,), (0,)))
                for q in range(2):
                    piece = slice(128 * q, 128 * q + 128)
                    attn_out[:, lanes_at(at + 128 * q)] = blended[:, piece].T.astype(BF16)
                    query_grad[:, lanes_at(at + 128 * q)] = turned[:, piece].T.astype(BF16)
            dks.append((dk[:WINDOW], dk[WINDOW:]))
            dvs.append((dv[:WINDOW], dv[WINDOW:]))
        own_k[:, lanes_at(p * 128)] = join_sides(dks, lo) * 0.125
        own_v[:, lanes_at(p * 128)] = join_sides(dvs, lo)
        return carry

    e_copies = []

    def send_back(n):
        total = give[rows_of(head), wide_at(n)].astype(F32)
        for (t, _), copy in zip(peers, d_copies[n]):
            copy.wait_recv()
            total = total + d_buf[n, t, :, : total.shape[1]].astype(F32)
        copies = []
        for s, who in earlier:
            e_send[n, s - 1] = jnp.where(tok - owner == s, total[:, :PART], 0.0).astype(BF16)
            copies.append(ship(e_send.at[n, s - 1], e_recv.at[n, s - 1], e_sems, LAG * n + s - 1, who))
        e_copies.append(copies)
        return total

    send_back(0)
    send_back(1)
    lax.fori_loop(0, 1, after, 0)
    send_back(2)
    total = send_back(3)
    sink_sum = total[:8, PART:] + total[8:, PART:]
    z_send[...] = sink_sum
    z_copies = [(t, ship(z_send, z_recv.at[t], z_sems, t, who)) for t, who in z_peers]
    back_copies.append(ship(near_send.at[:, keys_at], near_back.at[:, keys_at], n_sems, 3, left))
    lax.fori_loop(1, 3, after, 0)
    places = [tail_of(wrap(tok + s, RING), start, parent)[1] for s in range(1, LAG + 1)]

    f_copies = []

    def land(n):
        for copy in e_copies[n]:
            copy.wait_recv()
        arrived = [e_recv[n, s].astype(F32) for s in range(LAG)]

        def landed(place_):
            landing = jnp.zeros((ROWS, PART), F32)
            for s in range(LAG):
                landing = landing + jnp.where(places[s] == place_, arrived[s], 0.0)
            return landing.astype(BF16)

        for t, who in peers:
            f_send[n, t] = landed(who[1])
            f_copies.append(ship(f_send.at[n, t], f_recv.at[rows_of(head), chunk_at(n)], f_sems, GROUP * n + t, who))
        f_recv[rows_of(head), chunk_at(n)] = landed(head)

    land(0)
    land(1)
    lax.fori_loop(3, PAIRS, after, 0)
    land(2)
    land(3)
    for t, copy in z_copies:
        copy.wait_recv()
        sink_sum = sink_sum + z_recv[t]
    x_send[...] = sink_sum
    x_copies = [(t, ship(x_send, x_recv.at[t], x_sems, t, who)) for t, who in x_peers]
    for copy in back_copies:
        copy.wait_recv()
    own_k[...] = own_k[...] + near_back[:, :KV].astype(F32)
    own_v[...] = own_v[...] + near_back[:, KV:].astype(F32)
    for copy in f_copies:
        copy.wait_recv()
    key_grad[...] = (own_k[...] + f_recv[:, KV:].astype(F32)).astype(BF16)
    value_grad[...] = (own_v[...] + f_recv[:, :KV].astype(F32)).astype(BF16)
    for t, copy in x_copies:
        copy.wait_recv()
        sink_sum = sink_sum + x_recv[t]
    sums = jnp.sum(sink_sum, axis=1, keepdims=True)
    place_ = 4 * ((row >> 1) & 1) + 2 * (row >> 2) + (row & 1)
    line = jnp.sum(jnp.where(place_ == lane, sums, 0.0), axis=0)
    sink_grad[...] = -line[:8]
    for copy in sent:
        copy.wait_send()


def deliver(*refs):
    copies = [pltpu.make_async_copy(refs[n], refs[5 + n], refs[10].at[n]) for n in range(5)]
    for copy in copies:
        copy.start()
    for copy in copies:
        copy.wait()


RESULTS = (
    ((WINDOW, 4096), BF16),
    ((WINDOW, 4096), BF16),
    ((WINDOW, KV), BF16),
    ((WINDOW, KV), BF16),
    ((8,), F32),
)
VMEM = pl.BlockSpec(memory_space=pltpu.VMEM)
HBM = pl.BlockSpec(memory_space=pltpu.HBM)
DMA = pltpu.SemaphoreType.DMA


def local(queries, key_states, value_states, out_grad, sink_logits, branch_start, branch_len, parent_list):
    block = pltpu.VMEM((WINDOW, 2 * KV), BF16)
    slices = pltpu.VMEM((GROUP, ROWS, PART), BF16)
    lags = pltpu.VMEM((LAG, ROWS, PART), BF16)
    three = pltpu.VMEM((CHUNKS, LAG, ROWS, PART), BF16)
    rows = pltpu.VMEM((WINDOW, 4096), BF16)
    units = (PAIRS, 4, 2 * WINDOW, 256)
    turned = pltpu.VMEM((PAIRS, 4, 128, 256), BF16)
    results = pl.pallas_call(
        kernel,
        name="banded",
        out_shape=tuple(pltpu.VMEM(shape, kind) for shape, kind in RESULTS),
        in_specs=[HBM] * 8,
        out_specs=(VMEM,) * 5,
        scratch_shapes=[
            pltpu.SMEM((64,), jnp.int32), pltpu.SMEM((64,), jnp.int32),
            pltpu.SMEM((2, 64), jnp.int32), pltpu.SMEM((8,), F32),
            rows, rows,
            pltpu.VMEM((WINDOW, 2 * KV + 128), BF16),
            slices, slices, slices, pltpu.VMEM((GROUP, ROWS, PART + 128), BF16),
            block,
            three,
            lags, lags, lags, lags,
            pltpu.VMEM((CHUNKS, ROWS, PART), BF16),
            block, block,
            pltpu.VMEM((GROUP, 8, 128), F32),
            turned, turned,
            pltpu.VMEM(units, F32), pltpu.VMEM(units, F32),
            pltpu.VMEM(units, BF16), pltpu.VMEM(units, BF16),
            pltpu.VMEM((WINDOW, KV), F32), pltpu.VMEM((WINDOW, KV), F32),
            pltpu.VMEM((WINDOW, 2 * KV + 128), BF16),
            pltpu.VMEM((CHUNKS, GROUP, ROWS, PART + 128), BF16),
            block, block,
            three, three,
            pltpu.VMEM((CHUNKS, GROUP, ROWS, PART), BF16),
            block,
            pltpu.VMEM((8, 128), F32), pltpu.VMEM((Z, 8, 128), F32),
            pltpu.VMEM((8, 128), F32), pltpu.VMEM((X, 8, 128), F32),
            pltpu.VMEM((PAIRS, 8, 256), F32), pltpu.VMEM((PAIRS, 8, 256), F32),
            DMA((8,)),
            DMA((2, CHUNKS * GROUP)), DMA((2, 4)), DMA((2, CHUNKS * LAG)), DMA((2, CHUNKS * GROUP)),
            DMA((2, CHUNKS * GROUP)), DMA((2, CHUNKS * LAG)), DMA((2, CHUNKS * GROUP)), DMA((2, Z)), DMA((2, X)),
        ],
        compiler_params=pltpu.CompilerParams(
            collective_id=0, has_side_effects=True, vmem_limit_bytes=58 * 1024 * 1024
        ),
    )(
        *(
            pltpu.with_memory_space_constraint(x, pltpu.HBM)
            for x in (
                branch_start, branch_len, parent_list.T, sink_logits, queries, out_grad, key_states, value_states
            )
        ),
    )
    return pl.pallas_call(
        deliver,
        name="deliver",
        out_shape=tuple(jax.ShapeDtypeStruct(shape, kind) for shape, kind in RESULTS),
        in_specs=[VMEM] * 5,
        out_specs=(HBM,) * 5,
        scratch_shapes=[DMA((5,))],
    )(*(pltpu.with_memory_space_constraint(result, pltpu.VMEM) for result in results))


def solution(mesh):
    rows = P(("tok", "head"), None)
    return jax.shard_map(
        local,
        mesh=mesh,
        in_specs=(rows, rows, rows, rows, P("head"), P(), P(), P()),
        out_specs=(rows, rows, rows, rows, P("head")),
        check_vma=False,
    )
```

```python
import jax
import jax.numpy as jnp
from jax import lax
from jax.experimental import pallas as pl
from jax.experimental.pallas import tpu as pltpu
from jax.sharding import PartitionSpec as P

HEAD_DIM = 64
WINDOW = 128
LAG = 3
CHUNKS = 4
PART = 256
PAIRS = 4
BR_DEV = 2
GROUP = 8
RING = 32
ROWS = WINDOW // GROUP
KV = 512
Z = 8
X = 4
F32 = jnp.float32
BF16 = jnp.bfloat16
MESH = pl.DeviceIdType.MESH


def place():
    return lax.axis_index("tok"), lax.axis_index("head")


def block_state(tok, head, start, length, parent):
    pos = (tok * GROUP + head) * WINDOW
    alive, opening = False, False
    for b in range(BR_DEV):
        first = start[tok * BR_DEV + b]
        covers = (first <= pos) & (pos < first + length[tok * BR_DEV + b])
        alive = alive | covers
        opening = opening | (covers & (first == pos))
    return alive, opening, parent[0, tok * BR_DEV] >= 0


def tail_of(tok, start, parent):
    row = tok * BR_DEV
    token = start[jnp.maximum(parent[0, row], 0)] + parent[1, row]
    return lax.shift_right_logical(token, 10), lax.shift_right_logical(token, 7) & (GROUP - 1)


def send(src, dst, sems, slot, tok, head):
    copy = pltpu.make_async_remote_copy(
        src_ref=src,
        dst_ref=dst,
        send_sem=sems.at[0, slot],
        recv_sem=sems.at[1, slot],
        device_id=(tok, head),
        device_id_type=MESH,
    )
    copy.start()
    return copy


def wrap(value, count):
    return lax.rem(value + count, count)


def dot(left, right, dims):
    return lax.dot_general(left, right, (dims, ((), ())), preferred_element_type=F32)


def both_sides(block, lo):
    turned = pltpu.roll(block, HEAD_DIM, 1)
    zero = jnp.zeros_like(block)
    return (
        (jnp.where(lo, block, zero), jnp.where(lo, zero, turned)),
        (jnp.where(lo, turned, zero), jnp.where(lo, zero, block)),
    )


def join_sides(parts, lo):
    (a0, a1), (b0, b1) = parts
    return jnp.where(lo, a0, b1) + pltpu.roll(jnp.where(lo, b0, a1), HEAD_DIM, 1)


FAR_FIRST = (4, 5, 3, 6, 2, 7, 1)


def split_rows(rows):
    high = rows.astype(BF16).astype(F32)
    return jnp.concatenate([high, rows - high], 1).astype(BF16)


def kernel(
    start_in, length_in, parent_in, sink_in, queries, out_grad, keys, values,
    attn_out, query_grad, key_grad, value_grad, sink_grad,
    start, length, parent, sink, query, grad, pair, a0, a1, a2, a3, near, b_send, b0, b1, b2, b3, mine, tail, prev, table,
    q_turned, g_turned, s_own, p_own, probs, slopes, own_k, own_v,
    give, d_buf, near_send, near_back, e_send, e_recv, f_send, f_recv, z_send, z_recv, x_send, x_recv, part, lines,
    load_sems, a_sems, n_sems, b_sems, c_sems, d_sems, e_sems, f_sems, z_sems, x_sems,
):
    tok, head = place()
    x, z = tok // Z, lax.rem(tok, Z)
    peers = [(t, (tok, wrap(head + t, GROUP))) for t in FAR_FIRST]
    later = [(s, (wrap(tok + s, RING), head)) for s in (3, 2, 1)]
    earlier = [(s, (wrap(tok - s, RING), head)) for s in (3, 2, 1)]
    z_peers = [(t, (x * Z + wrap(z + t, Z), head)) for t in FAR_FIRST]
    x_peers = [(t, (wrap(x + t, X) * Z + z, head)) for t in (2, 3, 1)]
    right, left = (tok, wrap(head + 1, GROUP)), (tok, wrap(head - 1, GROUP))

    loads = [
        pltpu.make_async_copy(src, dst, load_sems.at[n])
        for n, (src, dst) in enumerate((
            (keys, pair.at[:, pl.ds(0, KV)]), (values, pair.at[:, pl.ds(KV, KV)]), (sink_in, sink), (start_in, start),
            (length_in, length), (parent_in, parent), (queries, query), (out_grad, grad),
        ))
    ]
    for load in loads:
        load.start()
    barrier = pltpu.get_barrier_semaphore()
    partners = [who for _, who in z_peers + later + earlier + peers + x_peers]
    for who in partners:
        pl.semaphore_signal(barrier, inc=1, device_id=who, device_id_type=MESH)

    for load in loads[2:6]:
        load.wait()
    alive, opening, rooted = block_state(tok, head, start, length, parent)
    ok = alive & (jnp.logical_not(opening) | rooted)
    outward = opening & rooted
    inward = alive & jnp.logical_not(opening)
    row = lax.broadcasted_iota(jnp.int32, (8, 128), 0)
    lane = lax.broadcasted_iota(jnp.int32, (8, 128), 1)
    sink_tile = jnp.zeros((8, 128), F32)
    for g in range(8):
        sink_tile = jnp.where(row == g, sink[g], sink_tile)
    table[head] = sink_tile
    pair[:, 2 * KV :] = split_rows(jnp.broadcast_to(sink_tile[None], (GROUP, 8, 128))).reshape(WINDOW, 128)
    loads[0].wait()
    loads[1].wait()
    pl.semaphore_wait(barrier, len(partners))

    def rows_of(place_):
        return pl.ds(pl.multiple_of(place_ * ROWS, ROWS), ROWS)

    sent = []

    def ship(src, dst, sems, slot, who):
        copy = send(src, dst, sems, slot, *who)
        sent.append(copy)
        return copy

    keys_at, values_at = pl.ds(0, KV), pl.ds(KV, KV)
    a_bufs, b_recvs = (a0, a1, a2, a3), (b0, b1, b2, b3)

    def chunk_at(n):
        return pl.ds(PART * n, PART)

    def wide_at(n):
        return pl.ds(PART * n, PART + 128 if n == CHUNKS - 1 else PART)

    a_copies = [
        [ship(pair.at[rows_of(who[1]), wide_at(n)], a_bufs[n].at[t], a_sems, GROUP * n + t, who) for t, who in peers]
        for n in range(CHUNKS)
    ]
    for n in range(CHUNKS):
        a_bufs[n][0] = pair[rows_of(head), wide_at(n)]

    lo = lax.broadcasted_iota(jnp.int32, (WINDOW, 128), 1) < HEAD_DIM
    place_j = lax.broadcasted_iota(jnp.int32, (WINDOW, 256), 0)
    place_i = lax.broadcasted_iota(jnp.int32, (WINDOW, 256), 1) & (WINDOW - 1)
    causal = place_j <= place_i
    causal16 = causal.astype(F32).astype(BF16)
    bias = jnp.where(ok, 0.0, -jnp.inf)

    def lanes_at(at, size=128):
        return pl.ds(pl.multiple_of(at, size), size)

    def sides(ref, p, factor):
        k = both_sides(ref[:, lanes_at(p * 128)].astype(F32) * factor, lo)
        v = both_sides(ref[:, lanes_at(KV + p * 128)].astype(F32), lo)
        return k, v

    def stacked(ref, at):
        return jnp.concatenate([ref[:, lanes_at(at)], ref[:, lanes_at(at + 128)]], 0)

    def both_rows(sides_):
        return jnp.concatenate([side.astype(BF16) for side in sides_], 0)

    def before(p, carry):
        wide = lanes_at(p * 1024, 1024)
        grad[:, wide] = jnp.where(alive, grad[:, wide], jnp.zeros((), BF16))
        k, v = sides(pair, p, 0.125)
        for c in range(2):
            k_rows, v_rows = both_rows(k[c]), both_rows(v[c])
            for half in range(2):
                at = p * 1024 + 512 * c + 256 * half
                for ref, turned_ref, rows, own in (
                    (query, q_turned, k_rows, s_own), (grad, g_turned, v_rows, p_own)
                ):
                    turned = jnp.concatenate([ref[:, lanes_at(at + 128 * q)].T for q in range(2)], 1)
                    turned_ref[p, 2 * c + half] = turned
                    own[p, 2 * c + half] = dot(rows, turned, ((1,), (0,)))
        return carry

    loads[6].wait()
    loads[7].wait()
    lax.fori_loop(0, PAIRS // 2, before, 0)

    tails = [(s, who, (head - tail_of(who[0], start, parent)[1]) & (GROUP - 1)) for s, who in later]

    b_copies = []
    for n in range(CHUNKS):
        for copy in a_copies[n]:
            copy.wait_recv()
        b_copies.append([])
        for s, who, slot in tails:
            b_send[n, s - 1] = a_bufs[n][slot][:, :PART]
            b_copies[n].append(ship(b_send.at[n, s - 1], b_recvs[n].at[s - 1], b_sems, LAG * n + s - 1, who))
    near_copies = [
        ship(pair.at[:, at], near.at[:, at], n_sems, n, right) for n, at in enumerate((keys_at, values_at))
    ]
    for t in range(1, GROUP):
        extra = a3[t, :, PART:].astype(F32)
        table[wrap(head - t, GROUP)] = extra[:8] + extra[8:]
    for h in range(GROUP):
        for line in range(4):
            first = 4 * (line // 2) + line % 2
            both = [table[h, first + 2 * q : first + 2 * q + 1, :] for q in range(2)]
            at = 4 * (h % 2) + line
            lines[h // 2, at : at + 1, :] = jnp.concatenate(both, 1)
    lax.fori_loop(PAIRS // 2, PAIRS, before, 0)
    owner, _ = tail_of(tok, start, parent)
    behind = jnp.clip(tok - owner - 1, 0, LAG - 1)

    c_copies = []
    for n in range(CHUNKS):
        for copy in b_copies[n]:
            copy.wait_recv()
        mine[n] = b_recvs[n][behind]
        tail[rows_of(head), chunk_at(n)] = mine[n]
        c_copies.append([
            ship(mine.at[n], tail.at[rows_of(head), chunk_at(n)], c_sems, GROUP * n + t, who) for t, who in peers
        ])

    def choose(n):
        if n % 2 == 0:
            near_copies[n // 2].wait_recv()
        for copy in c_copies[n]:
            copy.wait_recv()
        at = chunk_at(n)
        prev[:, at] = jnp.where(ok, jnp.where(opening, tail[:, at], near[:, at]), jnp.zeros((), BF16))

    def gather_from(n):
        return [
            ship(give.at[rows_of(who[1]), wide_at(n)], d_buf.at[n, t, :, pl.ds(0, PART + 128 if n == CHUNKS - 1 else PART)],
                 d_sems, GROUP * n + t, who)
            for t, who in peers
        ]

    zero16 = jnp.zeros((), BF16)

    def hand(p, block, give_at, near_at):
        block = block.astype(BF16)
        give[:, lanes_at(give_at + p * 128)] = jnp.where(outward, block, zero16)
        near_send[:, lanes_at(near_at + p * 128)] = jnp.where(inward, block, zero16)

    def weigh(p, carry):
        k = both_sides(prev[:, lanes_at(p * 128)].astype(F32) * 0.125, lo)
        dvs = []
        for c in range(2):
            k_rows = both_rows(k[c])
            dv = jnp.zeros((256, 128), F32)
            for half in range(2):
                unit = 2 * c + half
                g_rows = stacked(grad, p * 1024 + 512 * c + 256 * half)
                scores_both = dot(k_rows, q_turned[p, unit], ((1,), (0,)))
                behind16 = []
                for e in range(2):
                    at, line = slice(128 * e, 128 * e + 128), 2 * unit + e
                    scores = jnp.where(causal, s_own[p, unit, at], scores_both[at] + bias)
                    sinks = lines[p, line : line + 1, :]
                    peak = jnp.maximum(jnp.max(scores, axis=0, keepdims=True), sinks)
                    exps = jnp.exp(scores - peak)
                    sink_exp = jnp.exp(sinks - peak)
                    inverse = 1.0 / (jnp.sum(exps, axis=0, keepdims=True) + sink_exp)
                    prob = exps * inverse
                    s_own[p, unit, at] = prob
                    part[p, line : line + 1, :] = sink_exp * inverse
                    prob16 = prob.astype(BF16)
                    probs[p, unit, at] = prob16
                    behind16.append(prob16 - prob16 * causal16)
                dv = dv + dot(jnp.concatenate(behind16, 0), g_rows, ((1,), (0,)))
            dvs.append((dv[:WINDOW], dv[WINDOW:]))
        hand(p, join_sides(dvs, lo), 0, KV)
        return carry

    d_copies = []
    for n in range(2):
        choose(n)
        lax.fori_loop(2 * n, 2 * n + 2, weigh, 0)
        d_copies.append(gather_from(n))
    back_copies = [ship(near_send.at[:, values_at], near_back.at[:, values_at], n_sems, 2, left)]

    def incline(p, carry):
        v = both_sides(prev[:, lanes_at(KV + p * 128)].astype(F32), lo)
        dks = []
        for c in range(2):
            v_rows = both_rows(v[c])
            dk = jnp.zeros((256, 128), F32)
            for half in range(2):
                unit = 2 * c + half
                q_rows = stacked(query, p * 1024 + 512 * c + 256 * half)
                inner_both = dot(v_rows, g_turned[p, unit], ((1,), (0,)))
                behind16 = []
                for e in range(2):
                    at, line = slice(128 * e, 128 * e + 128), 2 * unit + e
                    inner = jnp.where(causal, p_own[p, unit, at], inner_both[at])
                    prob = s_own[p, unit, at]
                    weighed = prob * inner
                    delta = jnp.sum(weighed, axis=0, keepdims=True)
                    slope16 = (weighed - prob * delta).astype(BF16)
                    part[p, line : line + 1, :] = part[p, line : line + 1, :] * delta
                    slopes[p, unit, at] = slope16
                    behind16.append(slope16 - slope16 * causal16)
                dk = dk + dot(jnp.concatenate(behind16, 0), q_rows, ((1,), (0,)))
            dks.append((dk[:WINDOW], dk[WINDOW:]))
        hand(p, join_sides(dks, lo) * 0.125, KV, 0)
        return carry

    choose(2)
    lax.fori_loop(0, 2, incline, 0)
    d_copies.append(gather_from(2))
    choose(3)
    lax.fori_loop(2, PAIRS, incline, 0)
    terms = part[...].reshape(GROUP, 4, 256)
    terms = jnp.concatenate([terms[:, :, :128], terms[:, :, 128:]], 1)
    give[:, 2 * KV :] = split_rows(terms).reshape(WINDOW, 128)
    d_copies.append(gather_from(3))

    def after(p, carry):
        k_own, v_own = sides(pair, p, 0.125)
        k_prev, v_prev = sides(prev, p, 0.125)
        dks, dvs = [], []
        for c in range(2):
            k_all = jnp.concatenate([k_own[c][0], k_prev[c][0], k_own[c][1], k_prev[c][1]], 0)
            v_all = jnp.concatenate([v_own[c][0], v_prev[c][0], v_own[c][1], v_prev[c][1]], 0)
            k_turned = k_all.T.astype(BF16)
            v_turned = v_all.T.astype(BF16)
            dk, dv = jnp.zeros((256, 128), F32), jnp.zeros((256, 128), F32)
            for half in range(2):
                at, unit = p * 1024 + 512 * c + 256 * half, 2 * c + half
                q_rows, g_rows = stacked(query, at), stacked(grad, at)
                prob_all, slope_all, prob_own, slope_own = [], [], [], []
                for e in range(2):
                    prob16 = probs[p, unit, 128 * e : 128 * e + 128]
                    slope16 = slopes[p, unit, 128 * e : 128 * e + 128]
                    prob_own.append(prob16 * causal16)
                    slope_own.append(slope16 * causal16)
                    prob_all += [prob_own[e], prob16 - prob_own[e]]
                    slope_all += [slope_own[e], slope16 - slope_own[e]]
                dk = dk + dot(jnp.concatenate(slope_own, 0), q_rows, ((1,), (0,)))
                dv = dv + dot(jnp.concatenate(prob_own, 0), g_rows, ((1,), (0,)))
                blended = dot(v_turned, jnp.concatenate(prob_all, 0), ((1,), (0,)))
                blended = jnp.where(alive, blended, 0.0)
                turned = dot(k_turned, jnp.concatenate(slope_all, 0), ((1,), (0,)))
                for q in range(2):
                    piece = slice(128 * q, 128 * q + 128)
                    attn_out[:, lanes_at(at + 128 * q)] = blended[:, piece].T.astype(BF16)
                    query_grad[:, lanes_at(at + 128 * q)] = turned[:, piece].T.astype(BF16)
            dks.append((dk[:WINDOW], dk[WINDOW:]))
            dvs.append((dv[:WINDOW], dv[WINDOW:]))
        own_k[:, lanes_at(p * 128)] = join_sides(dks, lo) * 0.125
        own_v[:, lanes_at(p * 128)] = join_sides(dvs, lo)
        return carry

    e_copies = []

    def send_back(n):
        total = give[rows_of(head), wide_at(n)].astype(F32)
        for (t, _), copy in zip(peers, d_copies[n]):
            copy.wait_recv()
            total = total + d_buf[n, t, :, : total.shape[1]].astype(F32)
        copies = []
        for s, who in earlier:
            e_send[n, s - 1] = jnp.where(tok - owner == s, total[:, :PART], 0.0).astype(BF16)
            copies.append(ship(e_send.at[n, s - 1], e_recv.at[n, s - 1], e_sems, LAG * n + s - 1, who))
        e_copies.append(copies)
        return total

    send_back(0)
    send_back(1)
    lax.fori_loop(0, 1, after, 0)
    send_back(2)
    total = send_back(3)
    sink_sum = total[:8, PART:] + total[8:, PART:]
    z_send[...] = sink_sum
    z_copies = [(t, ship(z_send, z_recv.at[t], z_sems, t, who)) for t, who in z_peers]
    back_copies.append(ship(near_send.at[:, keys_at], near_back.at[:, keys_at], n_sems, 3, left))
    lax.fori_loop(1, 2, after, 0)
    places = [tail_of(wrap(tok + s, RING), start, parent)[1] for s in range(1, LAG + 1)]

    f_copies = []

    def land(n):
        for copy in e_copies[n]:
            copy.wait_recv()
        arrived = [e_recv[n, s].astype(F32) for s in range(LAG)]

        def landed(place_):
            landing = jnp.zeros((ROWS, PART), F32)
            for s in range(LAG):
                landing = landing + jnp.where(places[s] == place_, arrived[s], 0.0)
            return landing.astype(BF16)

        for t, who in peers:
            f_send[n, t] = landed(who[1])
            f_copies.append(ship(f_send.at[n, t], f_recv.at[rows_of(head), chunk_at(n)], f_sems, GROUP * n + t, who))
        f_recv[rows_of(head), chunk_at(n)] = landed(head)

    land(0)
    land(1)
    lax.fori_loop(2, 3, after, 0)
    land(2)
    land(3)
    for t, copy in z_copies:
        copy.wait_recv()
        sink_sum = sink_sum + z_recv[t]
    x_send[...] = sink_sum
    x_copies = [(t, ship(x_send, x_recv.at[t], x_sems, t, who)) for t, who in x_peers]
    lax.fori_loop(3, 4, after, 0)
    for copy in back_copies:
        copy.wait_recv()
    own_k[...] = own_k[...] + near_back[:, :KV].astype(F32)
    own_v[...] = own_v[...] + near_back[:, KV:].astype(F32)
    for copy in f_copies:
        copy.wait_recv()
    key_grad[...] = (own_k[...] + f_recv[:, KV:].astype(F32)).astype(BF16)
    value_grad[...] = (own_v[...] + f_recv[:, :KV].astype(F32)).astype(BF16)
    for t, copy in x_copies:
        copy.wait_recv()
        sink_sum = sink_sum + x_recv[t]
    sums = jnp.sum(sink_sum, axis=1, keepdims=True)
    place_ = 4 * ((row >> 1) & 1) + 2 * (row >> 2) + (row & 1)
    line = jnp.sum(jnp.where(place_ == lane, sums, 0.0), axis=0)
    sink_grad[...] = -line[:8]
    for copy in sent:
        copy.wait_send()


def deliver(*refs):
    copies = [pltpu.make_async_copy(refs[n], refs[5 + n], refs[10].at[n]) for n in range(5)]
    for copy in copies:
        copy.start()
    for copy in copies:
        copy.wait()


RESULTS = (
    ((WINDOW, 4096), BF16),
    ((WINDOW, 4096), BF16),
    ((WINDOW, KV), BF16),
    ((WINDOW, KV), BF16),
    ((8,), F32),
)
VMEM = pl.BlockSpec(memory_space=pltpu.VMEM)
HBM = pl.BlockSpec(memory_space=pltpu.HBM)
DMA = pltpu.SemaphoreType.DMA


def local(queries, key_states, value_states, out_grad, sink_logits, branch_start, branch_len, parent_list):
    block = pltpu.VMEM((WINDOW, 2 * KV), BF16)
    slices = pltpu.VMEM((GROUP, ROWS, PART), BF16)
    lags = pltpu.VMEM((LAG, ROWS, PART), BF16)
    three = pltpu.VMEM((CHUNKS, LAG, ROWS, PART), BF16)
    rows = pltpu.VMEM((WINDOW, 4096), BF16)
    units = (PAIRS, 4, 2 * WINDOW, 256)
    turned = pltpu.VMEM((PAIRS, 4, 128, 256), BF16)
    results = pl.pallas_call(
        kernel,
        name="banded",
        out_shape=tuple(pltpu.VMEM(shape, kind) for shape, kind in RESULTS),
        in_specs=[HBM] * 8,
        out_specs=(VMEM,) * 5,
        scratch_shapes=[
            pltpu.SMEM((64,), jnp.int32), pltpu.SMEM((64,), jnp.int32),
            pltpu.SMEM((2, 64), jnp.int32), pltpu.SMEM((8,), F32),
            rows, rows,
            pltpu.VMEM((WINDOW, 2 * KV + 128), BF16),
            slices, slices, slices, pltpu.VMEM((GROUP, ROWS, PART + 128), BF16),
            block,
            three,
            lags, lags, lags, lags,
            pltpu.VMEM((CHUNKS, ROWS, PART), BF16),
            block, block,
            pltpu.VMEM((GROUP, 8, 128), F32),
            turned, turned,
            pltpu.VMEM(units, F32), pltpu.VMEM(units, F32),
            pltpu.VMEM(units, BF16), pltpu.VMEM(units, BF16),
            pltpu.VMEM((WINDOW, KV), F32), pltpu.VMEM((WINDOW, KV), F32),
            pltpu.VMEM((WINDOW, 2 * KV + 128), BF16),
            pltpu.VMEM((CHUNKS, GROUP, ROWS, PART + 128), BF16),
            block, block,
            three, three,
            pltpu.VMEM((CHUNKS, GROUP, ROWS, PART), BF16),
            block,
            pltpu.VMEM((8, 128), F32), pltpu.VMEM((Z, 8, 128), F32),
            pltpu.VMEM((8, 128), F32), pltpu.VMEM((X, 8, 128), F32),
            pltpu.VMEM((PAIRS, 8, 256), F32), pltpu.VMEM((PAIRS, 8, 256), F32),
            DMA((8,)),
            DMA((2, CHUNKS * GROUP)), DMA((2, 4)), DMA((2, CHUNKS * LAG)), DMA((2, CHUNKS * GROUP)),
            DMA((2, CHUNKS * GROUP)), DMA((2, CHUNKS * LAG)), DMA((2, CHUNKS * GROUP)), DMA((2, Z)), DMA((2, X)),
        ],
        compiler_params=pltpu.CompilerParams(
            collective_id=0, has_side_effects=True, vmem_limit_bytes=58 * 1024 * 1024
        ),
    )(
        *(
            pltpu.with_memory_space_constraint(x, pltpu.HBM)
            for x in (
                branch_start, branch_len, parent_list.T, sink_logits, queries, out_grad, key_states, value_states
            )
        ),
    )
    return pl.pallas_call(
        deliver,
        name="deliver",
        out_shape=tuple(jax.ShapeDtypeStruct(shape, kind) for shape, kind in RESULTS),
        in_specs=[VMEM] * 5,
        out_specs=(HBM,) * 5,
        scratch_shapes=[DMA((5,))],
    )(*(pltpu.with_memory_space_constraint(result, pltpu.VMEM) for result in results))


def solution(mesh):
    rows = P(("tok", "head"), None)
    return jax.shard_map(
        local,
        mesh=mesh,
        in_specs=(rows, rows, rows, rows, P("head"), P(), P(), P()),
        out_specs=(rows, rows, rows, rows, P("head")),
        check_vma=False,
    )
```

```python
import jax
import jax.numpy as jnp
from jax import lax
from jax.experimental import pallas as pl
from jax.experimental.pallas import tpu as pltpu
from jax.sharding import PartitionSpec as P

HEAD_DIM = 64
WINDOW = 128
LAG = 3
CHUNKS = 4
PART = 256
PAIRS = 4
BR_DEV = 2
GROUP = 8
RING = 32
ROWS = WINDOW // GROUP
KV = 512
Z = 8
X = 4
F32 = jnp.float32
BF16 = jnp.bfloat16
MESH = pl.DeviceIdType.MESH


def place():
    return lax.axis_index("tok"), lax.axis_index("head")


def block_state(tok, head, start, length, parent):
    pos = (tok * GROUP + head) * WINDOW
    alive, opening = False, False
    for b in range(BR_DEV):
        first = start[tok * BR_DEV + b]
        covers = (first <= pos) & (pos < first + length[tok * BR_DEV + b])
        alive = alive | covers
        opening = opening | (covers & (first == pos))
    return alive, opening, parent[0, tok * BR_DEV] >= 0


def tail_of(tok, start, parent):
    row = tok * BR_DEV
    token = start[jnp.maximum(parent[0, row], 0)] + parent[1, row]
    return lax.shift_right_logical(token, 10), lax.shift_right_logical(token, 7) & (GROUP - 1)


def send(src, dst, sems, slot, tok, head):
    copy = pltpu.make_async_remote_copy(
        src_ref=src,
        dst_ref=dst,
        send_sem=sems.at[0, slot],
        recv_sem=sems.at[1, slot],
        device_id=(tok, head),
        device_id_type=MESH,
    )
    copy.start()
    return copy


def wrap(value, count):
    return lax.rem(value + count, count)


def dot(left, right, dims):
    return lax.dot_general(left, right, (dims, ((), ())), preferred_element_type=F32)


def both_sides(block, lo):
    turned = pltpu.roll(block, HEAD_DIM, 1)
    zero = jnp.zeros_like(block)
    return (
        (jnp.where(lo, block, zero), jnp.where(lo, zero, turned)),
        (jnp.where(lo, turned, zero), jnp.where(lo, zero, block)),
    )


def join_sides(parts, lo):
    (a0, a1), (b0, b1) = parts
    return jnp.where(lo, a0, b1) + pltpu.roll(jnp.where(lo, b0, a1), HEAD_DIM, 1)


FAR_FIRST = (4, 5, 3, 6, 2, 7, 1)


def split_rows(rows):
    high = rows.astype(BF16).astype(F32)
    return jnp.concatenate([high, rows - high], 1).astype(BF16)


def kernel(
    start_in, length_in, parent_in, sink_in, queries, out_grad, keys, values,
    attn_out, query_grad, key_grad, value_grad, sink_grad,
    start, length, parent, sink, query, grad, pair, a0, a1, a2, a3, near, b_send, b0, b1, b2, b3, mine, tail, prev, table,
    q_turned, g_turned, s_own, p_own, probs, slopes, own_k, own_v,
    give, d_buf, near_send, near_back, e_send, e_recv, f_send, f_recv, z_send, z_recv, x_send, x_recv, part, lines,
    load_sems, a_sems, n_sems, b_sems, c_sems, d_sems, e_sems, f_sems, z_sems, x_sems,
):
    tok, head = place()
    x, z = tok // Z, lax.rem(tok, Z)
    peers = [(t, (tok, wrap(head + t, GROUP))) for t in FAR_FIRST]
    later = [(s, (wrap(tok + s, RING), head)) for s in (3, 2, 1)]
    earlier = [(s, (wrap(tok - s, RING), head)) for s in (3, 2, 1)]
    z_peers = [(t, (x * Z + wrap(z + t, Z), head)) for t in FAR_FIRST]
    x_peers = [(t, (wrap(x + t, X) * Z + z, head)) for t in (2, 3, 1)]
    right, left = (tok, wrap(head + 1, GROUP)), (tok, wrap(head - 1, GROUP))

    loads = [
        pltpu.make_async_copy(src, dst, load_sems.at[n])
        for n, (src, dst) in enumerate((
            (keys, pair.at[:, pl.ds(0, KV)]), (values, pair.at[:, pl.ds(KV, KV)]), (sink_in, sink), (start_in, start),
            (length_in, length), (parent_in, parent), (queries, query), (out_grad, grad),
        ))
    ]
    for load in loads:
        load.start()
    barrier = pltpu.get_barrier_semaphore()
    partners = [who for _, who in z_peers + later + earlier + peers + x_peers]
    for who in partners:
        pl.semaphore_signal(barrier, inc=1, device_id=who, device_id_type=MESH)

    for load in loads[2:6]:
        load.wait()
    alive, opening, rooted = block_state(tok, head, start, length, parent)
    ok = alive & (jnp.logical_not(opening) | rooted)
    outward = opening & rooted
    inward = alive & jnp.logical_not(opening)
    row = lax.broadcasted_iota(jnp.int32, (8, 128), 0)
    lane = lax.broadcasted_iota(jnp.int32, (8, 128), 1)
    sink_tile = jnp.zeros((8, 128), F32)
    for g in range(8):
        sink_tile = jnp.where(row == g, sink[g], sink_tile)
    table[head] = sink_tile
    pair[:, 2 * KV :] = split_rows(jnp.broadcast_to(sink_tile[None], (GROUP, 8, 128))).reshape(WINDOW, 128)
    loads[0].wait()
    loads[1].wait()
    pl.semaphore_wait(barrier, len(partners))

    def rows_of(place_):
        return pl.ds(pl.multiple_of(place_ * ROWS, ROWS), ROWS)

    sent = []

    def ship(src, dst, sems, slot, who):
        copy = send(src, dst, sems, slot, *who)
        sent.append(copy)
        return copy

    keys_at, values_at = pl.ds(0, KV), pl.ds(KV, KV)
    a_bufs, b_recvs = (a0, a1, a2, a3), (b0, b1, b2, b3)

    def chunk_at(n):
        return pl.ds(PART * n, PART)

    def wide_at(n):
        return pl.ds(PART * n, PART + 128 if n == CHUNKS - 1 else PART)

    a_copies = [
        [ship(pair.at[rows_of(who[1]), wide_at(n)], a_bufs[n].at[t], a_sems, GROUP * n + t, who) for t, who in peers]
        for n in range(CHUNKS)
    ]
    for n in range(CHUNKS):
        a_bufs[n][0] = pair[rows_of(head), wide_at(n)]

    lo = lax.broadcasted_iota(jnp.int32, (WINDOW, 128), 1) < HEAD_DIM
    place_j = lax.broadcasted_iota(jnp.int32, (WINDOW, 256), 0)
    place_i = lax.broadcasted_iota(jnp.int32, (WINDOW, 256), 1) & (WINDOW - 1)
    causal = place_j <= place_i
    causal16 = causal.astype(F32).astype(BF16)
    bias = jnp.where(ok, 0.0, -jnp.inf)

    def lanes_at(at, size=128):
        return pl.ds(pl.multiple_of(at, size), size)

    def sides(ref, p, factor):
        k = both_sides(ref[:, lanes_at(p * 128)].astype(F32) * factor, lo)
        v = both_sides(ref[:, lanes_at(KV + p * 128)].astype(F32), lo)
        return k, v

    def stacked(ref, at):
        return jnp.concatenate([ref[:, lanes_at(at)], ref[:, lanes_at(at + 128)]], 0)

    def both_rows(sides_):
        return jnp.concatenate([side.astype(BF16) for side in sides_], 0)

    def before(p, carry):
        wide = lanes_at(p * 1024, 1024)
        grad[:, wide] = jnp.where(alive, grad[:, wide], jnp.zeros((), BF16))
        k, v = sides(pair, p, 0.125)
        for c in range(2):
            k_rows, v_rows = both_rows(k[c]), both_rows(v[c])
            for half in range(2):
                at = p * 1024 + 512 * c + 256 * half
                for ref, turned_ref, rows, own in (
                    (query, q_turned, k_rows, s_own), (grad, g_turned, v_rows, p_own)
                ):
                    turned = jnp.concatenate([ref[:, lanes_at(at + 128 * q)].T for q in range(2)], 1)
                    turned_ref[p, 2 * c + half] = turned
                    own[p, 2 * c + half] = dot(rows, turned, ((1,), (0,)))
        return carry

    loads[6].wait()
    loads[7].wait()
    lax.fori_loop(0, PAIRS // 2, before, 0)

    tails = [(s, who, (head - tail_of(who[0], start, parent)[1]) & (GROUP - 1)) for s, who in later]

    b_copies = []
    for n in range(CHUNKS):
        for copy in a_copies[n]:
            copy.wait_recv()
        b_copies.append([])
        for s, who, slot in tails:
            b_send[n, s - 1] = a_bufs[n][slot][:, :PART]
            b_copies[n].append(ship(b_send.at[n, s - 1], b_recvs[n].at[s - 1], b_sems, LAG * n + s - 1, who))
    near_copies = [
        ship(pair.at[:, at], near.at[:, at], n_sems, n, right) for n, at in enumerate((keys_at, values_at))
    ]
    for t in range(1, GROUP):
        extra = a3[t, :, PART:].astype(F32)
        table[wrap(head - t, GROUP)] = extra[:8] + extra[8:]
    for h in range(GROUP):
        for line in range(4):
            first = 4 * (line // 2) + line % 2
            both = [table[h, first + 2 * q : first + 2 * q + 1, :] for q in range(2)]
            at = 4 * (h % 2) + line
            lines[h // 2, at : at + 1, :] = jnp.concatenate(both, 1)
    lax.fori_loop(PAIRS // 2, PAIRS, before, 0)
    owner, _ = tail_of(tok, start, parent)
    behind = jnp.clip(tok - owner - 1, 0, LAG - 1)

    c_copies = []
    for n in range(CHUNKS):
        for copy in b_copies[n]:
            copy.wait_recv()
        mine[n] = b_recvs[n][behind]
        tail[rows_of(head), chunk_at(n)] = mine[n]
        c_copies.append([
            ship(mine.at[n], tail.at[rows_of(head), chunk_at(n)], c_sems, GROUP * n + t, who) for t, who in peers
        ])

    def choose(n):
        if n % 2 == 0:
            near_copies[n // 2].wait_recv()
        for copy in c_copies[n]:
            copy.wait_recv()
        at = chunk_at(n)
        prev[:, at] = jnp.where(ok, jnp.where(opening, tail[:, at], near[:, at]), jnp.zeros((), BF16))

    def gather_from(n):
        return [
            ship(give.at[rows_of(who[1]), wide_at(n)], d_buf.at[n, t, :, pl.ds(0, PART + 128 if n == CHUNKS - 1 else PART)],
                 d_sems, GROUP * n + t, who)
            for t, who in peers
        ]

    zero16 = jnp.zeros((), BF16)

    def hand(p, block, give_at, near_at):
        block = block.astype(BF16)
        give[:, lanes_at(give_at + p * 128)] = jnp.where(outward, block, zero16)
        near_send[:, lanes_at(near_at + p * 128)] = jnp.where(inward, block, zero16)

    def weigh(p, carry):
        k = both_sides(prev[:, lanes_at(p * 128)].astype(F32) * 0.125, lo)
        dvs = []
        for c in range(2):
            k_rows = both_rows(k[c])
            dv = jnp.zeros((256, 128), F32)
            for half in range(2):
                unit = 2 * c + half
                g_rows = stacked(grad, p * 1024 + 512 * c + 256 * half)
                scores_both = dot(k_rows, q_turned[p, unit], ((1,), (0,)))
                behind16 = []
                for e in range(2):
                    at, line = slice(128 * e, 128 * e + 128), 2 * unit + e
                    scores = jnp.where(causal, s_own[p, unit, at], scores_both[at] + bias)
                    sinks = lines[p, line : line + 1, :]
                    peak = jnp.maximum(jnp.max(scores, axis=0, keepdims=True), sinks)
                    exps = jnp.exp(scores - peak)
                    sink_exp = jnp.exp(sinks - peak)
                    inverse = 1.0 / (jnp.sum(exps, axis=0, keepdims=True) + sink_exp)
                    prob = exps * inverse
                    s_own[p, unit, at] = prob
                    part[p, line : line + 1, :] = sink_exp * inverse
                    prob16 = prob.astype(BF16)
                    probs[p, unit, at] = prob16
                    behind16.append(prob16 - prob16 * causal16)
                dv = dv + dot(jnp.concatenate(behind16, 0), g_rows, ((1,), (0,)))
            dvs.append((dv[:WINDOW], dv[WINDOW:]))
        hand(p, join_sides(dvs, lo), 0, KV)
        return carry

    d_copies = []
    for n in range(2):
        choose(n)
        lax.fori_loop(2 * n, 2 * n + 2, weigh, 0, unroll=True)
        d_copies.append(gather_from(n))
    back_copies = [ship(near_send.at[:, values_at], near_back.at[:, values_at], n_sems, 2, left)]

    def incline(p, carry):
        v = both_sides(prev[:, lanes_at(KV + p * 128)].astype(F32), lo)
        dks = []
        for c in range(2):
            v_rows = both_rows(v[c])
            dk = jnp.zeros((256, 128), F32)
            for half in range(2):
                unit = 2 * c + half
                q_rows = stacked(query, p * 1024 + 512 * c + 256 * half)
                inner_both = dot(v_rows, g_turned[p, unit], ((1,), (0,)))
                behind16 = []
                for e in range(2):
                    at, line = slice(128 * e, 128 * e + 128), 2 * unit + e
                    inner = jnp.where(causal, p_own[p, unit, at], inner_both[at])
                    prob = s_own[p, unit, at]
                    weighed = prob * inner
                    delta = jnp.sum(weighed, axis=0, keepdims=True)
                    slope16 = (weighed - prob * delta).astype(BF16)
                    part[p, line : line + 1, :] = part[p, line : line + 1, :] * delta
                    slopes[p, unit, at] = slope16
                    behind16.append(slope16 - slope16 * causal16)
                dk = dk + dot(jnp.concatenate(behind16, 0), q_rows, ((1,), (0,)))
            dks.append((dk[:WINDOW], dk[WINDOW:]))
        hand(p, join_sides(dks, lo) * 0.125, KV, 0)
        return carry

    choose(2)
    lax.fori_loop(0, 2, incline, 0, unroll=True)
    d_copies.append(gather_from(2))
    choose(3)
    lax.fori_loop(2, PAIRS, incline, 0, unroll=True)
    terms = part[...].reshape(GROUP, 4, 256)
    terms = jnp.concatenate([terms[:, :, :128], terms[:, :, 128:]], 1)
    give[:, 2 * KV :] = split_rows(terms).reshape(WINDOW, 128)
    d_copies.append(gather_from(3))

    def after(p, carry):
        k_own, v_own = sides(pair, p, 0.125)
        k_prev, v_prev = sides(prev, p, 0.125)
        dks, dvs = [], []
        for c in range(2):
            k_all = jnp.concatenate([k_own[c][0], k_prev[c][0], k_own[c][1], k_prev[c][1]], 0)
            v_all = jnp.concatenate([v_own[c][0], v_prev[c][0], v_own[c][1], v_prev[c][1]], 0)
            k_turned = k_all.T.astype(BF16)
            v_turned = v_all.T.astype(BF16)
            dk, dv = jnp.zeros((256, 128), F32), jnp.zeros((256, 128), F32)
            for half in range(2):
                at, unit = p * 1024 + 512 * c + 256 * half, 2 * c + half
                q_rows, g_rows = stacked(query, at), stacked(grad, at)
                prob_all, slope_all, prob_own, slope_own = [], [], [], []
                for e in range(2):
                    prob16 = probs[p, unit, 128 * e : 128 * e + 128]
                    slope16 = slopes[p, unit, 128 * e : 128 * e + 128]
                    prob_own.append(prob16 * causal16)
                    slope_own.append(slope16 * causal16)
                    prob_all += [prob_own[e], prob16 - prob_own[e]]
                    slope_all += [slope_own[e], slope16 - slope_own[e]]
                dk = dk + dot(jnp.concatenate(slope_own, 0), q_rows, ((1,), (0,)))
                dv = dv + dot(jnp.concatenate(prob_own, 0), g_rows, ((1,), (0,)))
                blended = dot(v_turned, jnp.concatenate(prob_all, 0), ((1,), (0,)))
                blended = jnp.where(alive, blended, 0.0)
                turned = dot(k_turned, jnp.concatenate(slope_all, 0), ((1,), (0,)))
                for q in range(2):
                    piece = slice(128 * q, 128 * q + 128)
                    attn_out[:, lanes_at(at + 128 * q)] = blended[:, piece].T.astype(BF16)
                    query_grad[:, lanes_at(at + 128 * q)] = turned[:, piece].T.astype(BF16)
            dks.append((dk[:WINDOW], dk[WINDOW:]))
            dvs.append((dv[:WINDOW], dv[WINDOW:]))
        own_k[:, lanes_at(p * 128)] = join_sides(dks, lo) * 0.125
        own_v[:, lanes_at(p * 128)] = join_sides(dvs, lo)
        return carry

    e_copies = []

    def send_back(n):
        total = give[rows_of(head), wide_at(n)].astype(F32)
        for (t, _), copy in zip(peers, d_copies[n]):
            copy.wait_recv()
            total = total + d_buf[n, t, :, : total.shape[1]].astype(F32)
        copies = []
        for s, who in earlier:
            e_send[n, s - 1] = jnp.where(tok - owner == s, total[:, :PART], 0.0).astype(BF16)
            copies.append(ship(e_send.at[n, s - 1], e_recv.at[n, s - 1], e_sems, LAG * n + s - 1, who))
        e_copies.append(copies)
        return total

    send_back(0)
    send_back(1)
    lax.fori_loop(0, 1, after, 0)
    send_back(2)
    total = send_back(3)
    sink_sum = total[:8, PART:] + total[8:, PART:]
    z_send[...] = sink_sum
    z_copies = [(t, ship(z_send, z_recv.at[t], z_sems, t, who)) for t, who in z_peers]
    back_copies.append(ship(near_send.at[:, keys_at], near_back.at[:, keys_at], n_sems, 3, left))
    lax.fori_loop(1, 2, after, 0)
    places = [tail_of(wrap(tok + s, RING), start, parent)[1] for s in range(1, LAG + 1)]

    f_copies = []

    def land(n):
        for copy in e_copies[n]:
            copy.wait_recv()
        arrived = [e_recv[n, s].astype(F32) for s in range(LAG)]

        def landed(place_):
            landing = jnp.zeros((ROWS, PART), F32)
            for s in range(LAG):
                landing = landing + jnp.where(places[s] == place_, arrived[s], 0.0)
            return landing.astype(BF16)

        for t, who in peers:
            f_send[n, t] = landed(who[1])
            f_copies.append(ship(f_send.at[n, t], f_recv.at[rows_of(head), chunk_at(n)], f_sems, GROUP * n + t, who))
        f_recv[rows_of(head), chunk_at(n)] = landed(head)

    land(0)
    land(1)
    lax.fori_loop(2, 3, after, 0)
    land(2)
    land(3)
    for t, copy in z_copies:
        copy.wait_recv()
        sink_sum = sink_sum + z_recv[t]
    x_send[...] = sink_sum
    x_copies = [(t, ship(x_send, x_recv.at[t], x_sems, t, who)) for t, who in x_peers]
    lax.fori_loop(3, 4, after, 0)
    for copy in back_copies:
        copy.wait_recv()
    own_k[...] = own_k[...] + near_back[:, :KV].astype(F32)
    own_v[...] = own_v[...] + near_back[:, KV:].astype(F32)
    for copy in f_copies:
        copy.wait_recv()
    key_grad[...] = (own_k[...] + f_recv[:, KV:].astype(F32)).astype(BF16)
    value_grad[...] = (own_v[...] + f_recv[:, :KV].astype(F32)).astype(BF16)
    for t, copy in x_copies:
        copy.wait_recv()
        sink_sum = sink_sum + x_recv[t]
    sums = jnp.sum(sink_sum, axis=1, keepdims=True)
    place_ = 4 * ((row >> 1) & 1) + 2 * (row >> 2) + (row & 1)
    line = jnp.sum(jnp.where(place_ == lane, sums, 0.0), axis=0)
    sink_grad[...] = -line[:8]
    for copy in sent:
        copy.wait_send()


def deliver(*refs):
    copies = [pltpu.make_async_copy(refs[n], refs[5 + n], refs[10].at[n]) for n in range(5)]
    for copy in copies:
        copy.start()
    for copy in copies:
        copy.wait()


RESULTS = (
    ((WINDOW, 4096), BF16),
    ((WINDOW, 4096), BF16),
    ((WINDOW, KV), BF16),
    ((WINDOW, KV), BF16),
    ((8,), F32),
)
VMEM = pl.BlockSpec(memory_space=pltpu.VMEM)
HBM = pl.BlockSpec(memory_space=pltpu.HBM)
DMA = pltpu.SemaphoreType.DMA


def local(queries, key_states, value_states, out_grad, sink_logits, branch_start, branch_len, parent_list):
    block = pltpu.VMEM((WINDOW, 2 * KV), BF16)
    slices = pltpu.VMEM((GROUP, ROWS, PART), BF16)
    lags = pltpu.VMEM((LAG, ROWS, PART), BF16)
    three = pltpu.VMEM((CHUNKS, LAG, ROWS, PART), BF16)
    rows = pltpu.VMEM((WINDOW, 4096), BF16)
    units = (PAIRS, 4, 2 * WINDOW, 256)
    turned = pltpu.VMEM((PAIRS, 4, 128, 256), BF16)
    results = pl.pallas_call(
        kernel,
        name="banded",
        out_shape=tuple(pltpu.VMEM(shape, kind) for shape, kind in RESULTS),
        in_specs=[HBM] * 8,
        out_specs=(VMEM,) * 5,
        scratch_shapes=[
            pltpu.SMEM((64,), jnp.int32), pltpu.SMEM((64,), jnp.int32),
            pltpu.SMEM((2, 64), jnp.int32), pltpu.SMEM((8,), F32),
            rows, rows,
            pltpu.VMEM((WINDOW, 2 * KV + 128), BF16),
            slices, slices, slices, pltpu.VMEM((GROUP, ROWS, PART + 128), BF16),
            block,
            three,
            lags, lags, lags, lags,
            pltpu.VMEM((CHUNKS, ROWS, PART), BF16),
            block, block,
            pltpu.VMEM((GROUP, 8, 128), F32),
            turned, turned,
            pltpu.VMEM(units, F32), pltpu.VMEM(units, F32),
            pltpu.VMEM(units, BF16), pltpu.VMEM(units, BF16),
            pltpu.VMEM((WINDOW, KV), F32), pltpu.VMEM((WINDOW, KV), F32),
            pltpu.VMEM((WINDOW, 2 * KV + 128), BF16),
            pltpu.VMEM((CHUNKS, GROUP, ROWS, PART + 128), BF16),
            block, block,
            three, three,
            pltpu.VMEM((CHUNKS, GROUP, ROWS, PART), BF16),
            block,
            pltpu.VMEM((8, 128), F32), pltpu.VMEM((Z, 8, 128), F32),
            pltpu.VMEM((8, 128), F32), pltpu.VMEM((X, 8, 128), F32),
            pltpu.VMEM((PAIRS, 8, 256), F32), pltpu.VMEM((PAIRS, 8, 256), F32),
            DMA((8,)),
            DMA((2, CHUNKS * GROUP)), DMA((2, 4)), DMA((2, CHUNKS * LAG)), DMA((2, CHUNKS * GROUP)),
            DMA((2, CHUNKS * GROUP)), DMA((2, CHUNKS * LAG)), DMA((2, CHUNKS * GROUP)), DMA((2, Z)), DMA((2, X)),
        ],
        compiler_params=pltpu.CompilerParams(
            collective_id=0, has_side_effects=True, vmem_limit_bytes=58 * 1024 * 1024
        ),
    )(
        *(
            pltpu.with_memory_space_constraint(x, pltpu.HBM)
            for x in (
                branch_start, branch_len, parent_list.T, sink_logits, queries, out_grad, key_states, value_states
            )
        ),
    )
    return pl.pallas_call(
        deliver,
        name="deliver",
        out_shape=tuple(jax.ShapeDtypeStruct(shape, kind) for shape, kind in RESULTS),
        in_specs=[VMEM] * 5,
        out_specs=(HBM,) * 5,
        scratch_shapes=[DMA((5,))],
    )(*(pltpu.with_memory_space_constraint(result, pltpu.VMEM) for result in results))


def solution(mesh):
    rows = P(("tok", "head"), None)
    return jax.shard_map(
        local,
        mesh=mesh,
        in_specs=(rows, rows, rows, rows, P("head"), P(), P(), P()),
        out_specs=(rows, rows, rows, rows, P("head")),
        check_vma=False,
    )
```

```python
import jax
import jax.numpy as jnp
from jax import lax
from jax.experimental import pallas as pl
from jax.experimental.pallas import tpu as pltpu
from jax.sharding import PartitionSpec as P

HEAD_DIM = 64
WINDOW = 128
LAG = 3
CHUNKS = 4
PART = 256
PAIRS = 4
BR_DEV = 2
GROUP = 8
RING = 32
ROWS = WINDOW // GROUP
KV = 512
Z = 8
X = 4
F32 = jnp.float32
BF16 = jnp.bfloat16
MESH = pl.DeviceIdType.MESH


def place():
    return lax.axis_index("tok"), lax.axis_index("head")


def block_state(tok, head, start, length, parent):
    pos = (tok * GROUP + head) * WINDOW
    alive, opening = False, False
    for b in range(BR_DEV):
        first = start[tok * BR_DEV + b]
        covers = (first <= pos) & (pos < first + length[tok * BR_DEV + b])
        alive = alive | covers
        opening = opening | (covers & (first == pos))
    return alive, opening, parent[0, tok * BR_DEV] >= 0


def tail_of(tok, start, parent):
    row = tok * BR_DEV
    token = start[jnp.maximum(parent[0, row], 0)] + parent[1, row]
    return lax.shift_right_logical(token, 10), lax.shift_right_logical(token, 7) & (GROUP - 1)


def send(src, dst, sems, slot, tok, head):
    copy = pltpu.make_async_remote_copy(
        src_ref=src,
        dst_ref=dst,
        send_sem=sems.at[0, slot],
        recv_sem=sems.at[1, slot],
        device_id=(tok, head),
        device_id_type=MESH,
    )
    copy.start()
    return copy


def wrap(value, count):
    return lax.rem(value + count, count)


def dot(left, right, dims):
    return lax.dot_general(left, right, (dims, ((), ())), preferred_element_type=F32)


def both_sides(block, lo):
    turned = pltpu.roll(block, HEAD_DIM, 1)
    zero = jnp.zeros_like(block)
    return (
        (jnp.where(lo, block, zero), jnp.where(lo, zero, turned)),
        (jnp.where(lo, turned, zero), jnp.where(lo, zero, block)),
    )


def join_sides(parts, lo):
    (a0, a1), (b0, b1) = parts
    return jnp.where(lo, a0, b1) + pltpu.roll(jnp.where(lo, b0, a1), HEAD_DIM, 1)


FAR_FIRST = (4, 5, 3, 6, 2, 7, 1)


def split_rows(rows):
    high = rows.astype(BF16).astype(F32)
    return jnp.concatenate([high, rows - high], 1).astype(BF16)


def kernel(
    start_in, length_in, parent_in, sink_in, queries, out_grad, keys, values,
    attn_out, query_grad, key_grad, value_grad, sink_grad,
    start, length, parent, sink, query, grad, pair, a0, a1, a2, a3, near, b_send, b0, b1, b2, b3, mine, tail, prev, table,
    q_turned, g_turned, s_own, p_own, probs, slopes, own_k, own_v,
    give, d_buf, near_send, near_back, e_send, e_recv, f_send, f_recv, z_send, z_recv, x_send, x_recv, part, lines,
    load_sems, a_sems, n_sems, b_sems, c_sems, d_sems, e_sems, f_sems, z_sems, x_sems,
):
    tok, head = place()
    x, z = tok // Z, lax.rem(tok, Z)
    peers = [(t, (tok, wrap(head + t, GROUP))) for t in FAR_FIRST]
    later = [(s, (wrap(tok + s, RING), head)) for s in (3, 2, 1)]
    earlier = [(s, (wrap(tok - s, RING), head)) for s in (3, 2, 1)]
    z_peers = [(t, (x * Z + wrap(z + t, Z), head)) for t in FAR_FIRST]
    x_peers = [(t, (wrap(x + t, X) * Z + z, head)) for t in (2, 3, 1)]
    right, left = (tok, wrap(head + 1, GROUP)), (tok, wrap(head - 1, GROUP))

    loads = [
        pltpu.make_async_copy(src, dst, load_sems.at[n])
        for n, (src, dst) in enumerate((
            (keys, pair.at[:, pl.ds(0, KV)]), (values, pair.at[:, pl.ds(KV, KV)]), (sink_in, sink), (start_in, start),
            (length_in, length), (parent_in, parent), (queries, query), (out_grad, grad),
        ))
    ]
    for load in loads:
        load.start()
    barrier = pltpu.get_barrier_semaphore()
    partners = [who for _, who in z_peers + later + earlier + peers + x_peers]
    for who in partners:
        pl.semaphore_signal(barrier, inc=1, device_id=who, device_id_type=MESH)

    for load in loads[2:6]:
        load.wait()
    alive, opening, rooted = block_state(tok, head, start, length, parent)
    ok = alive & (jnp.logical_not(opening) | rooted)
    outward = opening & rooted
    inward = alive & jnp.logical_not(opening)
    row = lax.broadcasted_iota(jnp.int32, (8, 128), 0)
    lane = lax.broadcasted_iota(jnp.int32, (8, 128), 1)
    sink_tile = jnp.zeros((8, 128), F32)
    for g in range(8):
        sink_tile = jnp.where(row == g, sink[g], sink_tile)
    table[head] = sink_tile
    pair[:, 2 * KV :] = split_rows(jnp.broadcast_to(sink_tile[None], (GROUP, 8, 128))).reshape(WINDOW, 128)
    loads[0].wait()
    loads[1].wait()
    pl.semaphore_wait(barrier, len(partners))

    def rows_of(place_):
        return pl.ds(pl.multiple_of(place_ * ROWS, ROWS), ROWS)

    sent = []

    def ship(src, dst, sems, slot, who):
        copy = send(src, dst, sems, slot, *who)
        sent.append(copy)
        return copy

    keys_at, values_at = pl.ds(0, KV), pl.ds(KV, KV)
    a_bufs, b_recvs = (a0, a1, a2, a3), (b0, b1, b2, b3)

    def chunk_at(n):
        return pl.ds(PART * n, PART)

    def wide_at(n):
        return pl.ds(PART * n, PART + 128 if n == CHUNKS - 1 else PART)

    a_copies = [
        [ship(pair.at[rows_of(who[1]), wide_at(n)], a_bufs[n].at[t], a_sems, GROUP * n + t, who) for t, who in peers]
        for n in range(CHUNKS)
    ]
    for n in range(CHUNKS):
        a_bufs[n][0] = pair[rows_of(head), wide_at(n)]

    lo = lax.broadcasted_iota(jnp.int32, (WINDOW, 128), 1) < HEAD_DIM
    place_j = lax.broadcasted_iota(jnp.int32, (WINDOW, 256), 0)
    place_i = lax.broadcasted_iota(jnp.int32, (WINDOW, 256), 1) & (WINDOW - 1)
    causal = place_j <= place_i
    causal16 = causal.astype(F32).astype(BF16)
    causal_both = (lax.broadcasted_iota(jnp.int32, (256, 256), 0) & (WINDOW - 1)) <= (
        lax.broadcasted_iota(jnp.int32, (256, 256), 1) & (WINDOW - 1)
    )
    back_seen = place_j > jnp.where(ok, place_i, WINDOW)

    def lanes_at(at, size=128):
        return pl.ds(pl.multiple_of(at, size), size)

    def sides(ref, p, factor):
        k = both_sides(ref[:, lanes_at(p * 128)].astype(F32) * factor, lo)
        v = both_sides(ref[:, lanes_at(KV + p * 128)].astype(F32), lo)
        return k, v

    def stacked(ref, at):
        return jnp.concatenate([ref[:, lanes_at(at)], ref[:, lanes_at(at + 128)]], 0)

    def both_rows(sides_):
        return jnp.concatenate([side.astype(BF16) for side in sides_], 0)

    def before(p, carry):
        wide = lanes_at(p * 1024, 1024)
        grad[:, wide] = jnp.where(alive, grad[:, wide], jnp.zeros((), BF16))
        k, v = sides(pair, p, 0.125)
        for c in range(2):
            k_rows, v_rows = both_rows(k[c]), both_rows(v[c])
            for half in range(2):
                at = p * 1024 + 512 * c + 256 * half
                for ref, turned_ref, rows, own in (
                    (query, q_turned, k_rows, s_own), (grad, g_turned, v_rows, p_own)
                ):
                    turned = jnp.concatenate([ref[:, lanes_at(at + 128 * q)].T for q in range(2)], 1)
                    turned_ref[p, 2 * c + half] = turned
                    product = dot(rows, turned, ((1,), (0,)))
                    if own is s_own:
                        product = jnp.where(causal_both, product, -jnp.inf)
                    own[p, 2 * c + half] = product
        return carry

    loads[6].wait()
    loads[7].wait()
    lax.fori_loop(0, PAIRS // 2, before, 0)

    tails = [(s, who, (head - tail_of(who[0], start, parent)[1]) & (GROUP - 1)) for s, who in later]

    b_copies = []
    for n in range(CHUNKS):
        for copy in a_copies[n]:
            copy.wait_recv()
        b_copies.append([])
        for s, who, slot in tails:
            b_send[n, s - 1] = a_bufs[n][slot][:, :PART]
            b_copies[n].append(ship(b_send.at[n, s - 1], b_recvs[n].at[s - 1], b_sems, LAG * n + s - 1, who))
    near_copies = [
        ship(pair.at[:, at], near.at[:, at], n_sems, n, right) for n, at in enumerate((keys_at, values_at))
    ]
    for t in range(1, GROUP):
        extra = a3[t, :, PART:].astype(F32)
        table[wrap(head - t, GROUP)] = extra[:8] + extra[8:]
    for h in range(GROUP):
        for line in range(4):
            first = 4 * (line // 2) + line % 2
            both = [table[h, first + 2 * q : first + 2 * q + 1, :] for q in range(2)]
            at = 4 * (h % 2) + line
            lines[h // 2, at : at + 1, :] = jnp.concatenate(both, 1)
    lax.fori_loop(PAIRS // 2, PAIRS, before, 0)
    owner, _ = tail_of(tok, start, parent)
    behind = jnp.clip(tok - owner - 1, 0, LAG - 1)

    c_copies = []
    for n in range(CHUNKS):
        for copy in b_copies[n]:
            copy.wait_recv()
        mine[n] = b_recvs[n][behind]
        tail[rows_of(head), chunk_at(n)] = mine[n]
        c_copies.append([
            ship(mine.at[n], tail.at[rows_of(head), chunk_at(n)], c_sems, GROUP * n + t, who) for t, who in peers
        ])

    def choose(n):
        if n % 2 == 0:
            near_copies[n // 2].wait_recv()
        for copy in c_copies[n]:
            copy.wait_recv()
        at = chunk_at(n)
        prev[:, at] = jnp.where(ok, jnp.where(opening, tail[:, at], near[:, at]), jnp.zeros((), BF16))

    def gather_from(n):
        return [
            ship(give.at[rows_of(who[1]), wide_at(n)], d_buf.at[n, t, :, pl.ds(0, PART + 128 if n == CHUNKS - 1 else PART)],
                 d_sems, GROUP * n + t, who)
            for t, who in peers
        ]

    zero16 = jnp.zeros((), BF16)

    def hand(p, block, give_at, near_at):
        block = block.astype(BF16)
        give[:, lanes_at(give_at + p * 128)] = jnp.where(outward, block, zero16)
        near_send[:, lanes_at(near_at + p * 128)] = jnp.where(inward, block, zero16)

    def weigh(p, carry):
        k = both_sides(prev[:, lanes_at(p * 128)].astype(F32) * 0.125, lo)
        dvs = []
        for c in range(2):
            k_rows = both_rows(k[c])
            dv = jnp.zeros((256, 128), F32)
            for half in range(2):
                unit = 2 * c + half
                g_rows = stacked(grad, p * 1024 + 512 * c + 256 * half)
                scores_both = dot(k_rows, q_turned[p, unit], ((1,), (0,)))
                behind16 = []
                for e in range(2):
                    at, line = slice(128 * e, 128 * e + 128), 2 * unit + e
                    scores = jnp.where(back_seen, scores_both[at], s_own[p, unit, at])
                    sinks = lines[p, line : line + 1, :]
                    peak = jnp.maximum(jnp.max(scores, axis=0, keepdims=True), sinks)
                    exps = jnp.exp(scores - peak)
                    sink_exp = jnp.exp(sinks - peak)
                    inverse = 1.0 / (jnp.sum(exps, axis=0, keepdims=True) + sink_exp)
                    prob = exps * inverse
                    s_own[p, unit, at] = prob
                    part[p, line : line + 1, :] = sink_exp * inverse
                    prob16 = prob.astype(BF16)
                    probs[p, unit, at] = prob16
                    behind16.append(prob16 - prob16 * causal16)
                dv = dv + dot(jnp.concatenate(behind16, 0), g_rows, ((1,), (0,)))
            dvs.append((dv[:WINDOW], dv[WINDOW:]))
        hand(p, join_sides(dvs, lo), 0, KV)
        return carry

    d_copies = []
    for n in range(2):
        choose(n)
        lax.fori_loop(2 * n, 2 * n + 2, weigh, 0, unroll=True)
        d_copies.append(gather_from(n))
    back_copies = [ship(near_send.at[:, values_at], near_back.at[:, values_at], n_sems, 2, left)]

    def incline(p, carry):
        v = both_sides(prev[:, lanes_at(KV + p * 128)].astype(F32), lo)
        dks = []
        for c in range(2):
            v_rows = both_rows(v[c])
            dk = jnp.zeros((256, 128), F32)
            for half in range(2):
                unit = 2 * c + half
                q_rows = stacked(query, p * 1024 + 512 * c + 256 * half)
                inner_both = dot(v_rows, g_turned[p, unit], ((1,), (0,)))
                behind16 = []
                for e in range(2):
                    at, line = slice(128 * e, 128 * e + 128), 2 * unit + e
                    inner = jnp.where(causal, p_own[p, unit, at], inner_both[at])
                    prob = s_own[p, unit, at]
                    weighed = prob * inner
                    delta = jnp.sum(weighed, axis=0, keepdims=True)
                    slope16 = (weighed - prob * delta).astype(BF16)
                    part[p, line : line + 1, :] = part[p, line : line + 1, :] * delta
                    slopes[p, unit, at] = slope16
                    behind16.append(slope16 - slope16 * causal16)
                dk = dk + dot(jnp.concatenate(behind16, 0), q_rows, ((1,), (0,)))
            dks.append((dk[:WINDOW], dk[WINDOW:]))
        hand(p, join_sides(dks, lo) * 0.125, KV, 0)
        return carry

    choose(2)
    lax.fori_loop(0, 2, incline, 0, unroll=True)
    d_copies.append(gather_from(2))
    choose(3)
    lax.fori_loop(2, PAIRS, incline, 0, unroll=True)
    terms = part[...].reshape(GROUP, 4, 256)
    terms = jnp.concatenate([terms[:, :, :128], terms[:, :, 128:]], 1)
    give[:, 2 * KV :] = split_rows(terms).reshape(WINDOW, 128)
    d_copies.append(gather_from(3))

    def after(p, carry):
        k_own, v_own = sides(pair, p, 0.125)
        k_prev, v_prev = sides(prev, p, 0.125)
        dks, dvs = [], []
        for c in range(2):
            k_all = jnp.concatenate([k_own[c][0], k_prev[c][0], k_own[c][1], k_prev[c][1]], 0)
            v_all = jnp.concatenate([v_own[c][0], v_prev[c][0], v_own[c][1], v_prev[c][1]], 0)
            k_turned = k_all.T.astype(BF16)
            v_turned = v_all.T.astype(BF16)
            dk, dv = jnp.zeros((256, 128), F32), jnp.zeros((256, 128), F32)
            for half in range(2):
                at, unit = p * 1024 + 512 * c + 256 * half, 2 * c + half
                q_rows, g_rows = stacked(query, at), stacked(grad, at)
                prob_all, slope_all, prob_own, slope_own = [], [], [], []
                for e in range(2):
                    prob16 = probs[p, unit, 128 * e : 128 * e + 128]
                    slope16 = slopes[p, unit, 128 * e : 128 * e + 128]
                    prob_own.append(prob16 * causal16)
                    slope_own.append(slope16 * causal16)
                    prob_all += [prob_own[e], prob16 - prob_own[e]]
                    slope_all += [slope_own[e], slope16 - slope_own[e]]
                dk = dk + dot(jnp.concatenate(slope_own, 0), q_rows, ((1,), (0,)))
                dv = dv + dot(jnp.concatenate(prob_own, 0), g_rows, ((1,), (0,)))
                blended = dot(v_turned, jnp.concatenate(prob_all, 0), ((1,), (0,)))
                blended = jnp.where(alive, blended, 0.0)
                turned = dot(k_turned, jnp.concatenate(slope_all, 0), ((1,), (0,)))
                for q in range(2):
                    piece = slice(128 * q, 128 * q + 128)
                    attn_out[:, lanes_at(at + 128 * q)] = blended[:, piece].T.astype(BF16)
                    query_grad[:, lanes_at(at + 128 * q)] = turned[:, piece].T.astype(BF16)
            dks.append((dk[:WINDOW], dk[WINDOW:]))
            dvs.append((dv[:WINDOW], dv[WINDOW:]))
        own_k[:, lanes_at(p * 128)] = join_sides(dks, lo) * 0.125
        own_v[:, lanes_at(p * 128)] = join_sides(dvs, lo)
        return carry

    e_copies = []

    def send_back(n):
        total = give[rows_of(head), wide_at(n)].astype(F32)
        for (t, _), copy in zip(peers, d_copies[n]):
            copy.wait_recv()
            total = total + d_buf[n, t, :, : total.shape[1]].astype(F32)
        copies = []
        for s, who in earlier:
            e_send[n, s - 1] = jnp.where(tok - owner == s, total[:, :PART], 0.0).astype(BF16)
            copies.append(ship(e_send.at[n, s - 1], e_recv.at[n, s - 1], e_sems, LAG * n + s - 1, who))
        e_copies.append(copies)
        return total

    send_back(0)
    send_back(1)
    lax.fori_loop(0, 1, after, 0)
    send_back(2)
    total = send_back(3)
    sink_sum = total[:8, PART:] + total[8:, PART:]
    z_send[...] = sink_sum
    z_copies = [(t, ship(z_send, z_recv.at[t], z_sems, t, who)) for t, who in z_peers]
    back_copies.append(ship(near_send.at[:, keys_at], near_back.at[:, keys_at], n_sems, 3, left))
    lax.fori_loop(1, 2, after, 0)
    places = [tail_of(wrap(tok + s, RING), start, parent)[1] for s in range(1, LAG + 1)]

    f_copies = []

    def land(n):
        for copy in e_copies[n]:
            copy.wait_recv()
        arrived = [e_recv[n, s].astype(F32) for s in range(LAG)]

        def landed(place_):
            landing = jnp.zeros((ROWS, PART), F32)
            for s in range(LAG):
                landing = landing + jnp.where(places[s] == place_, arrived[s], 0.0)
            return landing.astype(BF16)

        for t, who in peers:
            f_send[n, t] = landed(who[1])
            f_copies.append(ship(f_send.at[n, t], f_recv.at[rows_of(head), chunk_at(n)], f_sems, GROUP * n + t, who))
        f_recv[rows_of(head), chunk_at(n)] = landed(head)

    land(0)
    land(1)
    lax.fori_loop(2, 3, after, 0)
    land(2)
    land(3)
    for t, copy in z_copies:
        copy.wait_recv()
        sink_sum = sink_sum + z_recv[t]
    x_send[...] = sink_sum
    x_copies = [(t, ship(x_send, x_recv.at[t], x_sems, t, who)) for t, who in x_peers]
    lax.fori_loop(3, 4, after, 0)
    for copy in back_copies:
        copy.wait_recv()
    own_k[...] = own_k[...] + near_back[:, :KV].astype(F32)
    own_v[...] = own_v[...] + near_back[:, KV:].astype(F32)
    for copy in f_copies:
        copy.wait_recv()
    key_grad[...] = (own_k[...] + f_recv[:, KV:].astype(F32)).astype(BF16)
    value_grad[...] = (own_v[...] + f_recv[:, :KV].astype(F32)).astype(BF16)
    for t, copy in x_copies:
        copy.wait_recv()
        sink_sum = sink_sum + x_recv[t]
    sums = jnp.sum(sink_sum, axis=1, keepdims=True)
    place_ = 4 * ((row >> 1) & 1) + 2 * (row >> 2) + (row & 1)
    line = jnp.sum(jnp.where(place_ == lane, sums, 0.0), axis=0)
    sink_grad[...] = -line[:8]
    for copy in sent:
        copy.wait_send()


def deliver(*refs):
    copies = [pltpu.make_async_copy(refs[n], refs[5 + n], refs[10].at[n]) for n in range(5)]
    for copy in copies:
        copy.start()
    for copy in copies:
        copy.wait()


RESULTS = (
    ((WINDOW, 4096), BF16),
    ((WINDOW, 4096), BF16),
    ((WINDOW, KV), BF16),
    ((WINDOW, KV), BF16),
    ((8,), F32),
)
VMEM = pl.BlockSpec(memory_space=pltpu.VMEM)
HBM = pl.BlockSpec(memory_space=pltpu.HBM)
DMA = pltpu.SemaphoreType.DMA


def local(queries, key_states, value_states, out_grad, sink_logits, branch_start, branch_len, parent_list):
    block = pltpu.VMEM((WINDOW, 2 * KV), BF16)
    slices = pltpu.VMEM((GROUP, ROWS, PART), BF16)
    lags = pltpu.VMEM((LAG, ROWS, PART), BF16)
    three = pltpu.VMEM((CHUNKS, LAG, ROWS, PART), BF16)
    rows = pltpu.VMEM((WINDOW, 4096), BF16)
    units = (PAIRS, 4, 2 * WINDOW, 256)
    turned = pltpu.VMEM((PAIRS, 4, 128, 256), BF16)
    results = pl.pallas_call(
        kernel,
        name="banded",
        out_shape=tuple(pltpu.VMEM(shape, kind) for shape, kind in RESULTS),
        in_specs=[HBM] * 8,
        out_specs=(VMEM,) * 5,
        scratch_shapes=[
            pltpu.SMEM((64,), jnp.int32), pltpu.SMEM((64,), jnp.int32),
            pltpu.SMEM((2, 64), jnp.int32), pltpu.SMEM((8,), F32),
            rows, rows,
            pltpu.VMEM((WINDOW, 2 * KV + 128), BF16),
            slices, slices, slices, pltpu.VMEM((GROUP, ROWS, PART + 128), BF16),
            block,
            three,
            lags, lags, lags, lags,
            pltpu.VMEM((CHUNKS, ROWS, PART), BF16),
            block, block,
            pltpu.VMEM((GROUP, 8, 128), F32),
            turned, turned,
            pltpu.VMEM(units, F32), pltpu.VMEM(units, F32),
            pltpu.VMEM(units, BF16), pltpu.VMEM(units, BF16),
            pltpu.VMEM((WINDOW, KV), F32), pltpu.VMEM((WINDOW, KV), F32),
            pltpu.VMEM((WINDOW, 2 * KV + 128), BF16),
            pltpu.VMEM((CHUNKS, GROUP, ROWS, PART + 128), BF16),
            block, block,
            three, three,
            pltpu.VMEM((CHUNKS, GROUP, ROWS, PART), BF16),
            block,
            pltpu.VMEM((8, 128), F32), pltpu.VMEM((Z, 8, 128), F32),
            pltpu.VMEM((8, 128), F32), pltpu.VMEM((X, 8, 128), F32),
            pltpu.VMEM((PAIRS, 8, 256), F32), pltpu.VMEM((PAIRS, 8, 256), F32),
            DMA((8,)),
            DMA((2, CHUNKS * GROUP)), DMA((2, 4)), DMA((2, CHUNKS * LAG)), DMA((2, CHUNKS * GROUP)),
            DMA((2, CHUNKS * GROUP)), DMA((2, CHUNKS * LAG)), DMA((2, CHUNKS * GROUP)), DMA((2, Z)), DMA((2, X)),
        ],
        compiler_params=pltpu.CompilerParams(
            collective_id=0, has_side_effects=True, vmem_limit_bytes=58 * 1024 * 1024
        ),
    )(
        *(
            pltpu.with_memory_space_constraint(x, pltpu.HBM)
            for x in (
                branch_start, branch_len, parent_list.T, sink_logits, queries, out_grad, key_states, value_states
            )
        ),
    )
    return pl.pallas_call(
        deliver,
        name="deliver",
        out_shape=tuple(jax.ShapeDtypeStruct(shape, kind) for shape, kind in RESULTS),
        in_specs=[VMEM] * 5,
        out_specs=(HBM,) * 5,
        scratch_shapes=[DMA((5,))],
    )(*(pltpu.with_memory_space_constraint(result, pltpu.VMEM) for result in results))


def solution(mesh):
    rows = P(("tok", "head"), None)
    return jax.shard_map(
        local,
        mesh=mesh,
        in_specs=(rows, rows, rows, rows, P("head"), P(), P(), P()),
        out_specs=(rows, rows, rows, rows, P("head")),
        check_vma=False,
    )
```
